128 devices in a mesh: block: 8 (over x_lo, y), dp: 16 (over x_hi, z, core).
Axes of the slice: x: 4 (x_hi: 2, x_lo: 2; x = x_hi * 2 + x_lo), y: 4, z: 4, core: 2. Of those that a mesh axis runs over, the one named last changes fastest.
Arguments:
- inputs: bfloat16 [16, 3072, 1536], P('dp', 'block'), may hold values from -32 to 32
- w_query: bfloat16 [1536, 1536], replicated, may hold values from -0.25 to 0.25
- w_key: bfloat16 [1536, 1536], replicated, may hold values from -0.25 to 0.25
- w_value: bfloat16 [1536, 1536], replicated, may hold values from -0.15625 to 0.15625
- out_grad: bfloat16 [16, 3072, 1536], P('dp', 'block'), may hold values from -6 to 6
Outputs:
- input_grad: bfloat16 [16, 3072, 1536], P('dp', 'block')
- grad_query: float32 [1536, 1536], P('block')
- grad_key: float32 [1536, 1536], P('block')
- grad_value: float32 [1536, 1536], P('block')
The draws below stay inside these ranges and needn't reach their ends.
All inputs are finite; a program needn't handle non-finite values.
Results may differ from the reference program's by a relative error of at most 0.03.
Values may be sent and summed in bfloat16 or wider, within the bound.
No kernel may reach another device: no remote copies, remote signals or barrier semaphores. Data moves between devices by JAX's collectives and lax.ppermute only.
A program may use at most 192 MiB of HBM per device.

```python
import jax
import jax.numpy as jnp
from jax import lax

D = 1536
HEADS = 12
HEAD = 128
TOK = 384
BLOCKS = 8
ROLLOUTS = 16
SEQ = 3072


def shared_base(key):
    return jax.random.truncated_normal(key, -2.0, 2.0, (D, D), jnp.float32) * D ** (-0.5)


def draw_w_query(key, part):
    base = shared_base(key)
    return base.astype(jnp.bfloat16)


def draw_w_key(key, part):
    key = jax.random.fold_in(key, 12)
    fresh = jax.random.truncated_normal(key, -2.0, 2.0, (D, D), jnp.float32) * D ** (-0.5)
    mixed = fresh
    return mixed.astype(jnp.bfloat16)


def draw_inputs(key, part):
    key = jax.random.fold_in(key, 13)
    first_key = jax.random.fold_in(key, 0)
    shape = (ROLLOUTS, SEQ, D)
    base = jax.random.truncated_normal(first_key, -6.0, 6.0, shape, jnp.float32)
    result = base
    return result.astype(jnp.bfloat16)


def steps_of(rng, dims, pieces, least, high):
    loudness = 1.0
    for dim, shards_of in pieces:
        heights = jax.random.uniform(jax.random.fold_in(jax.random.fold_in(rng, 6), dim), (shards_of,), jnp.float32, least / len(pieces), high / len(pieces))
        loudness = loudness * jnp.repeat(jnp.exp(heights), dims[dim] // shards_of).reshape((-1,) + (1,) * (len(dims) - 1 - dim))
    return loudness


def gaussian(stream_key, dims, scale, bound, pieces=(), kind=jnp.bfloat16):
    level = steps_of(stream_key, dims, pieces, -0.22, 0.18) if pieces else 1.0
    drawn = jax.random.normal(stream_key, dims, jnp.float32) * scale * level
    return jnp.minimum(jnp.maximum(drawn, -bound), bound).astype(kind)


def setup_inputs(seed: int = 0) -> dict:
    key_of = jax.random.split(jax.random.key(seed), 6)
    inputs = draw_inputs(jax.random.fold_in(key_of[5], 71), 0)
    w_query = draw_w_query(jax.random.fold_in(key_of[5], 71), 0)
    w_key = draw_w_key(jax.random.fold_in(key_of[5], 71), 0)
    w_value = gaussian(key_of[3], (D, D), D ** -0.5, 0.15625)
    out_grad = gaussian(key_of[4], (ROLLOUTS, SEQ, D), 1.0, 6.0, ((0, 16), (1, 8)))
    return dict(inputs=inputs, w_query=w_query, w_key=w_key, w_value=w_value, out_grad=out_grad)


def rounded(values):
    return lax.optimization_barrier(values.astype(jnp.bfloat16)).astype(jnp.float32)


def window_grads(query, key, value, dout, index):
    scale = HEAD ** -0.5
    padding = jnp.zeros((2, TOK, HEADS, HEAD), jnp.bfloat16)
    key_pad = jnp.concatenate([padding, key], axis=0)
    value_pad = jnp.concatenate([padding, value], axis=0)
    key_win = lax.dynamic_slice_in_dim(key_pad, index, 3, 0).reshape(3 * TOK, HEADS, HEAD)
    value_win = lax.dynamic_slice_in_dim(value_pad, index, 3, 0).reshape(3 * TOK, HEADS, HEAD)
    query_now = lax.dynamic_index_in_dim(query, index, 0, keepdims=False)
    dout_now = lax.dynamic_index_in_dim(dout, index, 0, keepdims=False)
    valid = (index - 2 + jnp.arange(3 * TOK, dtype=jnp.int32) // TOK) >= 0
    scores = jnp.einsum('qhd,khd->hqk', query_now.astype(jnp.float32), key_win.astype(jnp.float32)) * scale
    scores = jnp.where(valid[None, None, :], scores, -1e30)
    peak = jnp.max(scores, axis=-1, keepdims=True)
    expo = jnp.exp(scores - peak)
    probs = expo / jnp.sum(expo, axis=-1, keepdims=True)
    probs_low = probs.astype(jnp.bfloat16)
    value_part = jnp.einsum('hqk,qhd->khd', probs_low.astype(jnp.float32), dout_now.astype(jnp.float32))
    dprobs = jnp.einsum('qhd,khd->hqk', dout_now.astype(jnp.float32), value_win.astype(jnp.float32))
    delta = jnp.sum(probs * dprobs, axis=-1, keepdims=True)
    dscores = (probs * (dprobs - delta) * scale).astype(jnp.bfloat16)
    query_grad = jnp.einsum('hqk,khd->qhd', dscores.astype(jnp.float32), key_win.astype(jnp.float32))
    key_part = jnp.einsum('hqk,qhd->khd', dscores.astype(jnp.float32), query_now.astype(jnp.float32))
    return (query_grad.astype(jnp.bfloat16).reshape(TOK, D), key_part.reshape(3, TOK, D), value_part.reshape(3, TOK, D))


def combine(parts):
    tail_one = jnp.zeros((1, TOK, D), jnp.float32)
    tail_two = jnp.zeros((2, TOK, D), jnp.float32)
    near = jnp.concatenate([rounded(parts[1:, 1]), tail_one], axis=0)
    far = jnp.concatenate([rounded(parts[2:, 0]), tail_two], axis=0)
    return (parts[:, 2] + near + far).astype(jnp.bfloat16)


def rollout(rows, dout, w_query, w_key, w_value):
    query = jnp.dot(rows, w_query, preferred_element_type=jnp.float32).astype(jnp.bfloat16)
    key = jnp.dot(rows, w_key, preferred_element_type=jnp.float32).astype(jnp.bfloat16)
    value = jnp.dot(rows, w_value, preferred_element_type=jnp.float32).astype(jnp.bfloat16)
    shape = (BLOCKS, TOK, HEADS, HEAD)
    query_h = query.reshape(shape)
    key_h = key.reshape(shape)
    value_h = value.reshape(shape)
    dout_h = dout.reshape(shape)

    def one_block(index):
        return window_grads(query_h, key_h, value_h, dout_h, index)

    query_grad, key_parts, value_parts = lax.map(one_block, jnp.arange(BLOCKS, dtype=jnp.int32))
    query_grad = query_grad.reshape(SEQ, D)
    key_grad = combine(key_parts).reshape(SEQ, D)
    value_grad = combine(value_parts).reshape(SEQ, D)
    input_grad = jnp.dot(query_grad, w_query.T, preferred_element_type=jnp.float32)
    input_grad = input_grad + jnp.dot(key_grad, w_key.T, preferred_element_type=jnp.float32)
    input_grad = input_grad + jnp.dot(value_grad, w_value.T, preferred_element_type=jnp.float32)
    stacked = jnp.concatenate([query_grad, key_grad, value_grad], axis=1)
    weight_grad = jnp.dot(rows.T, stacked, preferred_element_type=jnp.float32)
    return input_grad.astype(jnp.bfloat16), weight_grad


def reference(inputs, w_query, w_key, w_value, out_grad):
    def step(total, pair):
        input_grad, weight_grad = rollout(pair[0], pair[1], w_query, w_key, w_value)
        return total + weight_grad, input_grad

    start = jnp.zeros((D, 3 * D), jnp.float32)
    total, input_grad = lax.scan(step, start, (inputs, out_grad))
    return input_grad, total[:, :D], total[:, D:2 * D], total[:, 2 * D:]
```

```python
import jax
import jax.numpy as jnp
from jax import lax
from jax.experimental import pallas as pl
from jax.experimental.pallas import tpu as pltpu
from jax.sharding import Mesh, PartitionSpec as P

D = 1536
HEADS = 12
HEAD = 128
GROUP = HEADS // 4
COLS = GROUP * 3 * HEAD
SCALE = HEAD ** (-0.5)
LOG2E = 1.4426950408889634
BF = jnp.bfloat16
F32 = jnp.float32


def dot(a, b, ca, cb):
    return lax.dot_general(a, b, (((ca,), (cb,)), ((), ())), preferred_element_type=F32)


def attention_kernel(tok, bias_ref, qkv_ref, halo_ref, dout_ref, grads_ref, dhalo_ref, dk_ref, dv_ref):
    dk_ref[...] = jnp.zeros_like(dk_ref)
    dv_ref[...] = jnp.zeros_like(dv_ref)
    bias = bias_ref[0, 0]

    def rows(lo, hi, part):
        pieces = []
        if lo < 2:
            pieces.append(halo_ref[lo * tok : 2 * tok, (part - 1) * HEAD : part * HEAD])
        pieces.append(
            qkv_ref[max(lo - 2, 0) * tok : (hi - 2) * tok, part * HEAD : (part + 1) * HEAD]
        )
        return pieces[0] if len(pieces) == 1 else jnp.concatenate(pieces, axis=0)

    for i in range(4):
        here = slice(i * tok, (i + 1) * tok)
        win = slice(i * tok, (i + 3) * tok)
        q = qkv_ref[here, 0:HEAD]
        k = rows(i, i + 3, 1)
        v = rows(i, i + 3, 2)
        do = dout_ref[here, :]
        s = dot(k, q, 1, 1)
        if i < 2:
            edge = (2 - i) * tok
            s = jnp.concatenate([s[:edge] + bias, s[edge:]], axis=0)
        peak = jnp.max(s, axis=0, keepdims=True)
        e = jnp.exp2((s - peak) * (SCALE * LOG2E))
        p = e * (1.0 / jnp.sum(e, axis=0, keepdims=True))
        dv_ref[win, :] += dot(p.astype(BF), do, 1, 0)
        dp = dot(v, do, 1, 1)
        delta = jnp.sum(p * dp, axis=0, keepdims=True)
        ds = (p * (dp - delta) * SCALE).astype(BF)
        dk_ref[win, :] += dot(ds, q, 1, 0)
        dq = dot(k, ds, 0, 0)
        grads_ref[here, 0:HEAD] = dq.T.astype(BF)
    grads_ref[:, HEAD : 2 * HEAD] = dk_ref[2 * tok :, :].astype(BF)
    grads_ref[:, 2 * HEAD :] = dv_ref[2 * tok :, :].astype(BF)
    dhalo_ref[:, 0:HEAD] = dk_ref[: 2 * tok, :].astype(BF)
    dhalo_ref[:, HEAD:] = dv_ref[: 2 * tok, :].astype(BF)


def attention(bias, qkv, halo, dout):
    tok = qkv.shape[0] // 4
    return pl.pallas_call(
        lambda *refs: attention_kernel(tok, *refs),
        grid=(GROUP,),
        in_specs=[
            pl.BlockSpec(memory_space=pltpu.SMEM),
            pl.BlockSpec((4 * tok, 3 * HEAD), lambda h: (0, h)),
            pl.BlockSpec((2 * tok, 2 * HEAD), lambda h: (0, h)),
            pl.BlockSpec((4 * tok, HEAD), lambda h: (0, h)),
        ],
        out_specs=[
            pl.BlockSpec((4 * tok, 3 * HEAD), lambda h: (0, h)),
            pl.BlockSpec((2 * tok, 2 * HEAD), lambda h: (0, h)),
        ],
        out_shape=[
            jax.ShapeDtypeStruct(qkv.shape, BF),
            jax.ShapeDtypeStruct(halo.shape, BF),
        ],
        scratch_shapes=[
            pltpu.VMEM((6 * tok, HEAD), F32),
            pltpu.VMEM((6 * tok, HEAD), F32),
        ],
        compiler_params=pltpu.CompilerParams(vmem_limit_bytes=48 * 1024 * 1024),
        cost_estimate=pl.CostEstimate(
            flops=2 * 5 * 12 * 3 * tok * tok * HEAD * 2,
            bytes_accessed=6 * qkv.size,
            transcendentals=12 * 3 * tok * tok,
        ),
    )(bias, qkv, halo, dout)


def block_of(array, index, size):
    return lax.dynamic_slice_in_dim(array, index * size, size, 0)


def put(array, part, index):
    return lax.dynamic_update_slice_in_dim(array, part, index * part.shape[0], 0)


def on_device(sizes, inputs, w_query, w_key, w_value, out_grad):
    c = lax.axis_index("c")
    y = lax.axis_index("y")
    z = lax.axis_index("z")
    nz, nh = sizes["z"], sizes["xh"]
    tok = inputs.shape[1]
    half = tok // 2

    def ring(value, axis, steps, count=4):
        return lax.ppermute(value, axis, [(i, (i + steps) % count) for i in range(count)])

    def swap_sides(value):
        return lax.ppermute(value, ("xl", "c"), [(0, 0), (1, 2), (2, 1), (3, 3)])

    at = lambda steps: (y + steps) % 4

    rows = swap_sides(inputs[0])
    left = ring(rows, "y", 1)
    right = ring(rows, "y", -1)
    far_top = ring(left[:half], "y", 1)
    far_low = ring(right[half:], "y", -1)
    far = jnp.concatenate([far_top, far_low], axis=0)

    dout = swap_sides(out_grad[0])
    wide = GROUP * HEAD
    cols = lambda index: lax.dynamic_slice_in_dim(dout, index * wide, wide, 1)
    dout_all = jnp.zeros((4 * tok, wide), BF)
    dout_all = put(dout_all, cols(y), y)
    dout_all = put(dout_all, ring(cols(at(1)), "y", 1), at(-1))
    dout_all = put(dout_all, ring(cols(at(-1)), "y", -1), at(1))
    dout_all = put(dout_all, ring(cols(at(2)), "y", 2), at(2))

    weights = [
        lax.dynamic_slice_in_dim(w, y * wide, wide, 1).reshape(D, GROUP, HEAD)
        for w in (w_query, w_key, w_value)
    ]
    weight = jnp.stack(weights, axis=2).reshape(D, COLS)

    tokens = jnp.zeros((4 * tok, D), BF)
    qkv = jnp.zeros((4 * tok, COLS), BF)
    for part, index in ((rows, y), (left, at(-1)), (right, at(1)), (far, at(2))):
        tokens = put(tokens, part, index)
        qkv = put(qkv, dot(part, weight, 1, 0).astype(BF), index)

    halo = qkv[2 * tok :].reshape(2 * tok, GROUP, 3 * HEAD)[:, :, HEAD:]
    halo = halo.reshape(2 * tok, GROUP * 2 * HEAD)
    halo = lax.ppermute(halo, "c", [(0, 1)])
    bias = jnp.where(c == 0, -1e30, 0.0).astype(F32).reshape(1, 1)
    grads, dhalo = attention(bias, qkv, halo, dout_all)
    dhalo = lax.ppermute(dhalo, "c", [(1, 0)]).reshape(2 * tok, GROUP, 2 * HEAD)
    dhalo = jnp.pad(dhalo, ((2 * tok, 0), (0, 0), (HEAD, 0))).reshape(4 * tok, COLS)
    grads = (grads.astype(F32) + dhalo.astype(F32)).astype(BF)

    def partial(index):
        return dot(block_of(grads, index, tok), weight, 1, 1)

    part_far = partial(at(2)).astype(BF)
    back_top = ring(part_far[:half], "y", -1)
    back_low = ring(part_far[half:], "y", 1)

    half_d = D // 2
    columns = lambda index: lax.dynamic_slice_in_dim(tokens, index * half_d, half_d, 1)
    give = dot(columns(1 - c), grads, 0, 0).astype(BF)
    got = lax.ppermute(give, "c", [(0, 1), (1, 0)])

    part_left = partial(at(-1))
    part_right = partial(at(1))
    part_left = jnp.concatenate([part_left[:half] + back_top.astype(F32), part_left[half:]], axis=0)
    part_right = jnp.concatenate([part_right[:half], part_right[half:] + back_low.astype(F32)], axis=0)
    from_right = ring(part_left.astype(BF), "y", -1)
    from_left = ring(part_right.astype(BF), "y", 1)

    keep = dot(columns(c), grads, 0, 0)
    total = (keep + got.astype(F32)).astype(BF)
    fine = half_d // 4 // nz
    total = total.reshape(4, nz, fine, COLS)
    slab = lambda index: lax.dynamic_slice_in_dim(total, index % nz, 1, 1)[:, 0]
    share = slab(z).astype(F32)
    for steps in range(1, nz):
        share = share + ring(slab(z + steps), "z", steps, nz).astype(F32)
    share = share.astype(BF)

    def index_of(xl, xh, core):
        return (xl * nh + xh) * 2 + core

    def lane(xl, xh):
        return xh * 2 + xl

    around = 2 * nh
    summed = share.astype(F32)
    for steps in range(1, around):
        pairs = []
        for core in range(2):
            for xh in range(nh):
                source = (lane(core, xh) + steps) % around
                pairs.append(
                    (index_of(source % 2, source // 2, core), index_of(core, xh, core))
                )
        summed = summed + lax.ppermute(share, ("xl", "xh", "c"), pairs).astype(F32)
    summed = summed.astype(BF)

    def along(value, axis, steps, count):
        pairs = []
        for side in range(2):
            for i in range(count):
                j = (i + steps) % count
                pairs.append(((side * count + i) * 2 + side, (side * count + j) * 2 + side))
        return lax.ppermute(value, ("xl", axis, "c"), pairs)

    piece = lambda index: lax.dynamic_index_in_dim(summed, index % 4, 0, keepdims=False)
    gathered = jnp.zeros((4, fine, COLS), BF)
    gathered = lax.dynamic_update_index_in_dim(gathered, piece(y), y, 0)
    for steps in range(1, 4):
        gathered = lax.dynamic_update_index_in_dim(
            gathered, along(piece(y + steps), "y", steps, 4), at(-steps), 0
        )
    result = jnp.zeros((nz, 4, fine, COLS), BF)
    result = lax.dynamic_update_index_in_dim(result, gathered, z, 0)
    for steps in range(1, nz):
        result = lax.dynamic_update_index_in_dim(
            result, along(gathered, "z", steps, nz), (z - steps) % nz, 0
        )
    other = lax.ppermute(result, ("xl", "c"), [(0, 1), (3, 2)])
    result = jnp.where(lax.axis_index("xl") == c, result, other)
    result = result.reshape(nz, 4, fine, GROUP, 3, HEAD)
    outs = [
        result[:, :, :, :, part].transpose(0, 2, 1, 3, 4).reshape(nz * fine, D).astype(F32)
        for part in range(3)
    ]

    mine = partial(y) + from_right.astype(F32) + from_left.astype(F32)
    mine = swap_sides(mine.astype(BF))
    return mine[None], outs[0], outs[1], outs[2]


def solution(mesh):
    dp = mesh.shape["dp"]
    nz = 4 if dp == 16 else 1
    nh = dp // 2 // nz
    sizes = {"xl": 2, "y": 4, "xh": nh, "z": nz, "c": 2}
    fine = Mesh(mesh.devices.reshape(tuple(sizes.values())), tuple(sizes))
    block, rollouts = ("xl", "y"), ("xh", "z", "c")
    placed = (P(rollouts, block, None), P(), P(), P(), P(rollouts, block, None))
    return jax.shard_map(
        lambda *arrays: on_device(sizes, *arrays),
        mesh=fine,
        in_specs=placed,
        out_specs=(P(rollouts, block, None), P(block, None), P(block, None), P(block, None)),
        check_vma=False,
    )
```

```python
import jax
import jax.numpy as jnp
from jax import lax
from jax.experimental import pallas as pl
from jax.experimental.pallas import tpu as pltpu
from jax.sharding import Mesh, PartitionSpec as P

D = 1536
HEADS = 12
HEAD = 128
GROUP = HEADS // 4
COLS = GROUP * 3 * HEAD
SCALE = HEAD ** (-0.5)
LOG2E = 1.4426950408889634
BF = jnp.bfloat16
F32 = jnp.float32


def dot(a, b, ca, cb):
    return lax.dot_general(a, b, (((ca,), (cb,)), ((), ())), preferred_element_type=F32)


def attention_kernel(tok, bias_ref, q_ref, kv_ref, halo_ref, dout_ref, dq_ref, dkv_ref, dhalo_ref, acc_ref):
    bias = bias_ref[0, 0]
    zero = jnp.zeros((tok, HEAD), BF)

    def first(i):
        here = slice(i * tok, (i + 1) * tok)
        kv = kv_ref[max(i - 2, 0) * tok : (i + 1) * tok, :]
        if i < 2:
            kv = jnp.concatenate([halo_ref[i * tok : 2 * tok, :], kv], axis=0)
        qd = jnp.concatenate(
            [
                jnp.concatenate([q_ref[here, :], zero], axis=1),
                jnp.concatenate([zero, dout_ref[here, :]], axis=1),
            ],
            axis=0,
        )
        return kv, qd, dot(kv, qd, 1, 1)

    def second(i, kv, qd, both):
        s = both[:, :tok]
        dp = both[:, tok:]
        if i < 2:
            edge = (2 - i) * tok
            s = jnp.concatenate([s[:edge] + bias, s[edge:]], axis=0)
        peak = jnp.max(s, axis=0, keepdims=True) * (SCALE * LOG2E)
        e = jnp.exp2(s * (SCALE * LOG2E) - peak)
        p = e * (1.0 / jnp.sum(e, axis=0, keepdims=True))
        delta = jnp.sum(p * dp, axis=0, keepdims=True)
        ds = (p * (dp - delta)).astype(BF)
        dkv = dot(jnp.concatenate([ds, p.astype(BF)], axis=1), qd, 1, 0)
        for j in range(3):
            rows = slice((i + j) * tok, (i + j + 1) * tok)
            part = dkv[j * tok : (j + 1) * tok]
            if i == 0 or j == 2:
                acc_ref[rows, :] = part
            else:
                acc_ref[rows, :] += part
        dq = dot(kv[:, :HEAD], ds, 0, 0).T * SCALE
        dq_ref[i * tok : (i + 1) * tok, :] = dq.astype(BF)

    ahead = first(0)
    for i in range(4):
        now = ahead
        if i < 3:
            ahead = first(i + 1)
        second(i, *now)
    dkv_ref[:, :HEAD] = (acc_ref[2 * tok :, :HEAD] * SCALE).astype(BF)
    dkv_ref[:, HEAD:] = acc_ref[2 * tok :, HEAD:].astype(BF)
    dhalo_ref[:, :HEAD] = (acc_ref[: 2 * tok, :HEAD] * SCALE).astype(BF)
    dhalo_ref[:, HEAD:] = acc_ref[: 2 * tok, HEAD:].astype(BF)


def attention(bias, q, kv, halo, dout):
    tok = q.shape[0] // 4
    one = pl.BlockSpec((4 * tok, HEAD), lambda h: (0, h))
    two = pl.BlockSpec((4 * tok, 2 * HEAD), lambda h: (0, h))
    edge = pl.BlockSpec((2 * tok, 2 * HEAD), lambda h: (0, h))
    return pl.pallas_call(
        lambda *refs: attention_kernel(tok, *refs),
        grid=(GROUP,),
        in_specs=[pl.BlockSpec(memory_space=pltpu.SMEM), one, two, edge, one],
        out_specs=[one, two, edge],
        out_shape=[
            jax.ShapeDtypeStruct(q.shape, BF),
            jax.ShapeDtypeStruct(kv.shape, BF),
            jax.ShapeDtypeStruct(halo.shape, BF),
        ],
        scratch_shapes=[pltpu.VMEM((6 * tok, 2 * HEAD), F32)],
        compiler_params=pltpu.CompilerParams(vmem_limit_bytes=48 * 1024 * 1024),
        cost_estimate=pl.CostEstimate(
            flops=2 * 5 * 4 * GROUP * 3 * tok * tok * HEAD * 2,
            bytes_accessed=12 * kv.size,
            transcendentals=4 * GROUP * 3 * tok * tok,
        ),
    )(bias, q, kv, halo, dout)


def slabs_kernel(nz, place_ref, keep_kv_ref, keep_q_ref, got_kv_ref, got_q_ref, *outs):
    fine = keep_kv_ref.shape[0] // nz
    both = keep_kv_ref.shape[1]
    for steps in range(nz):
        at = pl.multiple_of(lax.rem(place_ref[0] + steps, nz) * fine, 16)
        rows = pl.ds(at, fine)
        total = keep_kv_ref[rows, :].astype(F32) + got_kv_ref[rows, :].astype(F32)
        outs[steps][0, :, :both] = total.astype(BF)
        total = keep_q_ref[rows, :].astype(F32) + got_q_ref[rows, :].astype(F32)
        outs[steps][0, :, both:] = total.astype(BF)


def make_slabs(place, nz, keep_kv, keep_q, got_kv, got_q):
    rows = keep_kv.shape[0] // 4
    shape = (4, rows // nz, COLS)
    spec = lambda array: pl.BlockSpec((rows, array.shape[1]), lambda n, place: (n, 0))
    return pl.pallas_call(
        lambda *refs: slabs_kernel(nz, *refs),
        grid_spec=pltpu.PrefetchScalarGridSpec(
            num_scalar_prefetch=1,
            grid=(4,),
            in_specs=[spec(keep_kv), spec(keep_q), spec(got_kv), spec(got_q)],
            out_specs=[pl.BlockSpec((1,) + shape[1:], lambda n, place: (n, 0, 0))] * nz,
        ),
        out_shape=[jax.ShapeDtypeStruct(shape, BF)] * nz,
        compiler_params=pltpu.CompilerParams(vmem_limit_bytes=32 * 1024 * 1024),
        cost_estimate=pl.CostEstimate(
            flops=keep_kv.size, bytes_accessed=9 * keep_kv.size, transcendentals=0
        ),
    )(place, keep_kv, keep_q, got_kv, got_q)


def block_of(array, index, size):
    return lax.dynamic_slice_in_dim(array, index * size, size, 0)


def put(array, part, index):
    return lax.dynamic_update_slice_in_dim(array, part, index * part.shape[0], 0)


def on_device(sizes, inputs, w_query, w_key, w_value, out_grad):
    c = lax.axis_index("c")
    y = lax.axis_index("y")
    z = lax.axis_index("z")
    xl = lax.axis_index("xl")
    nz, nh = sizes["z"], sizes["xh"]
    tok = inputs.shape[1]
    half = tok // 2
    home = xl == c

    def ring(value, axis, steps, count=4):
        return lax.ppermute(value, axis, [(i, (i + steps) % count) for i in range(count)])

    def side_ring(value, axis, steps, count, own):
        pairs = []
        for side in range(2):
            core = side if own else 1 - side
            for i in range(count):
                j = (i + steps) % count
                pairs.append(((side * count + i) * 2 + core, (side * count + j) * 2 + core))
        return lax.ppermute(value, ("xl", axis, "c"), pairs)

    def swap_sides(value):
        return lax.ppermute(value, ("xl", "c"), [(1, 2), (2, 1)])

    at = lambda steps: (y + steps) % 4
    wide = GROUP * HEAD

    def crossed(value, steps):
        pairs = []
        for side in range(2):
            for i in range(4):
                for core in range(2):
                    there = ((core * 4 + (i + steps) % 4) * 2) + side
                    if steps or side != core:
                        pairs.append(((side * 4 + i) * 2 + core, there))
        return lax.ppermute(value, ("xl", "y", "c"), pairs)

    own = inputs[0]
    cols = lambda index: lax.dynamic_slice_in_dim(out_grad[0], index * wide, wide, 1)
    moved = swap_sides(own)
    left_home = side_ring(own, "y", 1, 4, True)
    right_home = side_ring(own, "y", -1, 4, True)
    left_away = side_ring(moved, "y", 1, 4, False)
    right_away = side_ring(moved, "y", -1, 4, False)
    rows = jnp.where(home, own, moved)
    dout_own = cols(y)
    dout_own = jnp.where(home, dout_own, crossed(dout_own, 0))
    dout_left = crossed(cols(at(1)), 1)
    dout_right = crossed(cols(at(-1)), -1)
    dout_far = crossed(cols(at(2)), 2)
    dout_all = jnp.zeros((4 * tok, wide), BF)
    for part, index in ((dout_own, y), (dout_left, at(-1)), (dout_right, at(1)), (dout_far, at(2))):
        dout_all = put(dout_all, part, index)
    left_away, right_away, dout_all = lax.optimization_barrier((left_away, right_away, dout_all))
    left = jnp.where(home, left_home, left_away)
    right = jnp.where(home, right_home, right_away)
    far_top = ring(left[:half], "y", 1)
    far_low = ring(right[half:], "y", -1)

    slices = [lax.dynamic_slice_in_dim(w, y * wide, wide, 1) for w in (w_query, w_key, w_value)]
    weight_q = slices[0]
    weight_kv = jnp.concatenate(
        [slices[1 + part][:, h * HEAD : (h + 1) * HEAD] for h in range(GROUP) for part in range(2)],
        axis=1,
    )

    tokens = jnp.zeros((4 * tok, D), BF)
    kv = jnp.zeros((4 * tok, 2 * wide), BF)
    q = jnp.zeros((4 * tok, wide), BF)

    def place(tokens, kv, q, part, index):
        tokens = put(tokens, part, index)
        kv = put(kv, dot(part, weight_kv, 1, 0).astype(BF), index)
        q = put(q, dot(part, weight_q, 1, 0).astype(BF), index)
        return tokens, kv, q

    for part, index in ((rows, y), (left, at(-1)), (right, at(1))):
        tokens, kv, q = place(tokens, kv, q, part, index)
    tokens, kv, q, far_top, far_low = lax.optimization_barrier((tokens, kv, q, far_top, far_low))
    far = jnp.concatenate([far_top, far_low], axis=0)
    tokens, kv, q = place(tokens, kv, q, far, at(2))

    halo = lax.ppermute(kv[2 * tok :], "c", [(0, 1)])
    bias = jnp.where(c == 0, -1e30, 0.0).astype(F32).reshape(1, 1)
    dq, dkv, dhalo = attention(bias, q, kv, halo, dout_all)
    dhalo = lax.ppermute(dhalo, "c", [(1, 0)])

    half_d = D // 2
    columns = lambda index: lax.dynamic_slice_in_dim(tokens, index * half_d, half_d, 1)
    swap_cores = lambda value: lax.ppermute(value, "c", [(0, 1), (1, 0)])
    give_q = dot(columns(1 - c), dq, 0, 0).astype(BF)
    keep_q = dot(columns(c), dq, 0, 0).astype(BF)
    got_q = swap_cores(give_q)
    dhalo, keep_q = lax.optimization_barrier((dhalo, keep_q))
    upper = (dkv[2 * tok :].astype(F32) + dhalo.astype(F32)).astype(BF)
    dkv = lax.dynamic_update_slice_in_dim(dkv, upper, 2 * tok, 0)
    give_kv = dot(columns(1 - c), dkv, 0, 0).astype(BF)
    got_kv = swap_cores(give_kv)
    dkv, give_kv = lax.optimization_barrier((dkv, give_kv))

    def partial(index):
        return dot(block_of(dq, index, tok), weight_q, 1, 1) + dot(
            block_of(dkv, index, tok), weight_kv, 1, 1
        )

    part_far = partial(at(2)).astype(BF)
    back_top = ring(part_far[:half], "y", -1)
    back_low = ring(part_far[half:], "y", 1)
    dkv, part_far = lax.optimization_barrier((dkv, part_far))
    keep_kv = dot(columns(c), dkv, 0, 0).astype(BF)
    slabs = make_slabs(z.reshape(1), nz, keep_kv, keep_q, got_kv, got_q)
    fine = half_d // 4 // nz
    dkv, dq, *slabs = lax.optimization_barrier((dkv, dq, *slabs))
    sent = [ring(slabs[steps], "z", steps, nz) for steps in range(1, nz)]

    part_left = partial(at(-1))
    part_right = partial(at(1))
    part_left = jnp.concatenate([part_left[:half] + back_top.astype(F32), part_left[half:]], axis=0)
    part_right = jnp.concatenate([part_right[:half], part_right[half:] + back_low.astype(F32)], axis=0)
    part_left = part_left.astype(BF)
    part_right = part_right.astype(BF)
    *sent, part_left, part_right = lax.optimization_barrier((*sent, part_left, part_right))
    share = slabs[0].astype(F32)
    for part in sent:
        share = share + part.astype(F32)
    share = share.astype(BF)
    from_right = ring(part_left, "y", -1)
    from_left = ring(part_right, "y", 1)

    around = 2 * nh
    arrived = []
    for steps in range(1, around):
        pairs = []
        for core in range(2):
            for xh in range(nh):
                source = (xh * 2 + core + steps) % around
                pairs.append(
                    (((source % 2) * nh + source // 2) * 2 + core, (core * nh + xh) * 2 + core)
                )
        arrived.append(lax.ppermute(share, ("xl", "xh", "c"), pairs))
    *arrived, from_left, from_right = lax.optimization_barrier((*arrived, from_left, from_right))
    summed = share.astype(F32)
    for part in arrived:
        summed = summed + part.astype(F32)
    summed = summed.astype(BF)
    input_grad = partial(y) + from_left.astype(F32) + from_right.astype(F32)
    input_grad = input_grad.astype(BF)
    away_grad = swap_sides(input_grad)

    piece = lambda index: lax.dynamic_index_in_dim(summed, index % 4, 0, keepdims=False)
    gathered = jnp.zeros((3, fine, D), BF)

    def spread(gathered, piece, index):
        column = lambda i: piece[:, i * HEAD : (i + 1) * HEAD]
        parts = [
            [column(2 * GROUP + h) for h in range(GROUP)],
            [column(2 * h) for h in range(GROUP)],
            [column(2 * h + 1) for h in range(GROUP)],
        ]
        parts = jnp.stack([jnp.concatenate(part, axis=1) for part in parts])
        return lax.dynamic_update_slice_in_dim(gathered, parts, index * wide, 2)

    gathered = spread(gathered, piece(y), y)
    for steps in range(1, 4):
        gathered = spread(gathered, side_ring(piece(y + steps), "y", steps, 4, True), at(-steps))
    result = jnp.zeros((3, nz * fine, D), BF)
    result = lax.dynamic_update_slice_in_dim(result, gathered, z * fine, 1)
    for steps in range(1, nz):
        result = lax.dynamic_update_slice_in_dim(
            result, side_ring(gathered, "z", steps, nz, True), (z - steps) % nz * fine, 1
        )
    result, away_grad = lax.optimization_barrier((result, away_grad))
    other = lax.ppermute(result, ("xl", "c"), [(0, 1), (3, 2)])
    input_grad = jnp.where(home, input_grad, away_grad)
    outs = [jnp.where(home, result[part], other[part]).astype(F32) for part in range(3)]
    return input_grad[None], outs[0], outs[1], outs[2]


def solution(mesh):
    dp = mesh.shape["dp"]
    nz = 4 if dp == 16 else 1
    nh = dp // 2 // nz
    sizes = {"xl": 2, "y": 4, "xh": nh, "z": nz, "c": 2}
    fine = Mesh(mesh.devices.reshape(tuple(sizes.values())), tuple(sizes))
    block, rollouts = ("xl", "y"), ("xh", "z", "c")
    placed = (P(rollouts, block, None), P(), P(), P(), P(rollouts, block, None))
    return jax.shard_map(
        lambda *arrays: on_device(sizes, *arrays),
        mesh=fine,
        in_specs=placed,
        out_specs=(P(rollouts, block, None), P(block, None), P(block, None), P(block, None)),
        check_vma=False,
    )
```

```python
import jax
import jax.numpy as jnp
from jax import lax
from jax.experimental import pallas as pl
from jax.experimental.pallas import tpu as pltpu
from jax.sharding import Mesh, PartitionSpec as P

D = 1536
HEADS = 12
HEAD = 128
GROUP = HEADS // 4
COLS = GROUP * 3 * HEAD
SCALE = HEAD ** (-0.5)
LOG2E = 1.4426950408889634
FIRST = 2**40
BF = jnp.bfloat16
F32 = jnp.float32


def dot(a, b, ca, cb):
    return lax.dot_general(a, b, (((ca,), (cb,)), ((), ())), preferred_element_type=F32)


def attention_kernel(
    tok, nz, place_ref, bias_ref, q_ref, kv_ref, halo_ref, dout_ref, turned_ref,
    dq_ref, dkv_ref, dhalo_ref, give_ref, keep_ref, low_ref, high_ref,
    acc_ref, held_ref, grad_ref, sem_ref,
):
    step = pl.program_id(0)
    fetch = pltpu.make_async_copy(turned_ref, held_ref, sem_ref)

    @pl.when(step == 0)
    def _():
        fetch.start()

    bias = bias_ref[0, 0]
    zero = jnp.zeros((tok, HEAD), BF)

    def first(i):
        here = slice(i * tok, (i + 1) * tok)
        kv = kv_ref[max(i - 2, 0) * tok : (i + 1) * tok, :]
        if i < 2:
            kv = jnp.concatenate([halo_ref[i * tok : 2 * tok, :], kv], axis=0)
        qd = jnp.concatenate(
            [
                jnp.concatenate([q_ref[here, :], zero], axis=1),
                jnp.concatenate([zero, dout_ref[here, :]], axis=1),
            ],
            axis=0,
        )
        return kv, qd, dot(kv, qd, 1, 1)

    def second(i, kv, qd, both):
        s = both[:, :tok]
        dp = both[:, tok:]
        if i < 2:
            edge = (2 - i) * tok
            s = jnp.concatenate([s[:edge] + bias, s[edge:]], axis=0)
        peak = jnp.max(s, axis=0, keepdims=True) * (SCALE * LOG2E)
        e = jnp.exp2(s * (SCALE * LOG2E) - peak)
        p = e * (1.0 / jnp.sum(e, axis=0, keepdims=True))
        delta = jnp.sum(p * dp, axis=0, keepdims=True)
        ds = (p * (dp - delta)).astype(BF)
        dkv = dot(jnp.concatenate([ds, p.astype(BF)], axis=1), qd, 1, 0)
        for j in range(3):
            rows = slice((i + j) * tok, (i + j + 1) * tok)
            part = dkv[j * tok : (j + 1) * tok]
            if i == 0 or j == 2:
                acc_ref[rows, :] = part
            else:
                acc_ref[rows, :] += part
        dq = dot(kv[:, :HEAD], ds, 0, 0).T * SCALE
        dq_ref[i * tok : (i + 1) * tok, :] = dq.astype(BF)

    ahead = first(0)
    for i in range(4):
        now = ahead
        if i < 3:
            ahead = first(i + 1)
        second(i, *now)
    dkv_ref[:, :HEAD] = (acc_ref[2 * tok :, :HEAD] * SCALE).astype(BF)
    dkv_ref[:, HEAD:] = acc_ref[2 * tok :, HEAD:].astype(BF)
    dhalo_ref[:, :HEAD] = (acc_ref[: 2 * tok, :HEAD] * SCALE).astype(BF)
    dhalo_ref[:, HEAD:] = acc_ref[: 2 * tok, HEAD:].astype(BF)

    @pl.when(step == 0)
    def _():
        fetch.wait()
        low_ref[...] = held_ref[: D // 2, 2 * tok :]
        high_ref[...] = held_ref[D // 2 :, 2 * tok :]

    grad_ref[:, : 2 * HEAD] = dot(held_ref[...], dkv_ref[...], 1, 0)
    grad_ref[:, 2 * HEAD :] = dot(held_ref[...], dq_ref[...], 1, 0)
    fine = D // 8 // nz
    for out_ref, side in ((give_ref, 1 - place_ref[0]), (keep_ref, place_ref[0])):
        for steps in range(nz):
            for y in range(4):
                start = side * (D // 2) + (y * nz + lax.rem(place_ref[1] + steps, nz)) * fine
                rows = pl.ds(pl.multiple_of(start, 16), fine)
                out_ref[steps, y] = grad_ref[rows, :].astype(BF)


def attention(place, bias, q, kv, halo, dout, turned, nz):
    tok = q.shape[0] // 4
    one = pl.BlockSpec((4 * tok, HEAD), lambda h, place: (0, h))
    two = pl.BlockSpec((4 * tok, 2 * HEAD), lambda h, place: (0, h))
    edge = pl.BlockSpec((2 * tok, 2 * HEAD), lambda h, place: (0, h))
    corner = pl.BlockSpec((D // 2, 2 * tok), lambda h, place: (0, 0))
    shape = (nz, 4, D // 8 // nz, COLS)
    slabs = pl.BlockSpec(shape[:3] + (3 * HEAD,), lambda h, place: (0, 0, 0, h))
    made = lambda shape: jax.ShapeDtypeStruct(shape, BF)
    return pl.pallas_call(
        lambda *refs: attention_kernel(tok, nz, *refs),
        grid_spec=pltpu.PrefetchScalarGridSpec(
            num_scalar_prefetch=1,
            grid=(GROUP,),
            in_specs=[
                pl.BlockSpec(memory_space=pltpu.SMEM), one, two, edge, one,
                pl.BlockSpec(memory_space=pl.ANY),
            ],
            out_specs=[one, two, edge, slabs, slabs, corner, corner],
            scratch_shapes=[
                pltpu.VMEM((6 * tok, 2 * HEAD), F32),
                pltpu.VMEM((D, 4 * tok), BF),
                pltpu.VMEM((D, 3 * HEAD), F32),
                pltpu.SemaphoreType.DMA,
            ],
        ),
        out_shape=[
            made(q.shape), made(kv.shape), made(halo.shape), made(shape), made(shape),
            made((D // 2, 2 * tok)), made((D // 2, 2 * tok)),
        ],
        compiler_params=pltpu.CompilerParams(vmem_limit_bytes=60 * 1024 * 1024),
        cost_estimate=pl.CostEstimate(
            flops=2 * 5 * 4 * GROUP * 3 * tok * tok * HEAD * 2 + 8 * tok * D * COLS,
            bytes_accessed=24 * kv.size,
            transcendentals=4 * GROUP * 3 * tok * tok,
        ),
    )(place, bias, q, kv, halo, dout, turned)


def pick_kernel(place_ref, query_ref, key_ref, value_ref, q_ref, kv_ref):
    q_ref[...] = query_ref[...]
    kv_ref[:, :HEAD] = key_ref[...]
    kv_ref[:, HEAD:] = value_ref[...]


def pick_weights(index, w_query, w_key, w_value):
    piece = pl.BlockSpec((D, HEAD), lambda h, place: (0, place[0] * GROUP + h))
    return pl.pallas_call(
        pick_kernel,
        grid_spec=pltpu.PrefetchScalarGridSpec(
            num_scalar_prefetch=1,
            grid=(GROUP,),
            in_specs=[piece, piece, piece],
            out_specs=[
                pl.BlockSpec((D, HEAD), lambda h, place: (0, h)),
                pl.BlockSpec((D, 2 * HEAD), lambda h, place: (0, h)),
            ],
        ),
        out_shape=[
            jax.ShapeDtypeStruct((D, GROUP * HEAD), BF),
            jax.ShapeDtypeStruct((D, 2 * GROUP * HEAD), BF),
        ],
        compiler_params=pltpu.CompilerParams(vmem_limit_bytes=60 * 1024 * 1024),
        cost_estimate=pl.CostEstimate(
            flops=FIRST, bytes_accessed=4 * D * COLS, transcendentals=0
        ),
    )(index.reshape(1), w_query, w_key, w_value)


def place_kernel(split, place_ref, a_ref, b_ref, wkv_ref, wq_ref, *refs):
    t_ref, kv_ref, q_ref, block_ref = refs[-4:]
    step = pl.program_id(0)

    @pl.when(step == 0)
    def _():
        if split:
            half = a_ref.shape[0]
            block_ref[:half, :] = a_ref[...]
            block_ref[half:, :] = b_ref[...]
        else:
            block_ref[...] = a_ref[...]

            @pl.when(place_ref[1] == 0)
            def _():
                block_ref[...] = b_ref[...]

    block = block_ref[...]
    kv_ref[...] = dot(block, wkv_ref[...], 1, 0).astype(BF)
    q_ref[...] = dot(block, wq_ref[...], 1, 0).astype(BF)
    third = D // GROUP
    t_ref[...] = block_ref[:, pl.ds(pl.multiple_of(step * third, 128), third)].T


def place_block(buffers, a, b, home, index, weight_kv, weight_q, split=False):
    tok = a.shape[0] * (2 if split else 1)
    shapes = ((D, 4 * tok), (4 * tok, 2 * GROUP * HEAD), (4 * tok, GROUP * HEAD))
    whole = pl.BlockSpec(a.shape, lambda h, place: (0, 0))
    anywhere = pl.BlockSpec(memory_space=pl.ANY)
    return pl.pallas_call(
        lambda *refs: place_kernel(split, *refs),
        grid_spec=pltpu.PrefetchScalarGridSpec(
            num_scalar_prefetch=1,
            grid=(GROUP,),
            in_specs=[
                whole, whole,
                pl.BlockSpec((D, 2 * HEAD), lambda h, place: (0, h)),
                pl.BlockSpec((D, HEAD), lambda h, place: (0, h)),
            ]
            + [anywhere] * len(buffers),
            out_specs=[
                pl.BlockSpec((D // GROUP, tok), lambda h, place: (h, place[0])),
                pl.BlockSpec((tok, 2 * HEAD), lambda h, place: (place[0], h)),
                pl.BlockSpec((tok, HEAD), lambda h, place: (place[0], h)),
            ],
            scratch_shapes=[pltpu.VMEM((tok, D), BF)],
        ),
        out_shape=[jax.ShapeDtypeStruct(shape, BF) for shape in shapes],
        input_output_aliases={5: 0, 6: 1, 7: 2} if buffers else {},
        compiler_params=pltpu.CompilerParams(vmem_limit_bytes=60 * 1024 * 1024),
        cost_estimate=pl.CostEstimate(
            flops=FIRST, bytes_accessed=8 * tok * D, transcendentals=0
        ),
    )(jnp.stack([index, home.astype(jnp.int32)]), a, b, weight_kv, weight_q, *buffers)


def finish_kernel(nz, place_ref, keep_ref, got_ref, low_ref, high_ref, near_ref, far_ref, *refs):
    outs, acc_ref = refs[:-1], refs[-1]
    first = place_ref[0] == 0

    @pl.when(first)
    def _():
        acc_ref[...] = dot(low_ref[...], far_ref[...], 1, 0)

    @pl.when(jnp.logical_not(first))
    def _():
        acc_ref[...] = dot(high_ref[...], near_ref[...], 1, 0)

    fine = acc_ref.shape[0] // nz
    for steps in range(nz):
        at = pl.multiple_of(lax.rem(place_ref[1] + steps, nz) * fine, 16)
        total = keep_ref[steps, 0].astype(F32) + got_ref[steps, 0].astype(F32)
        part = acc_ref[pl.ds(at, fine), :]
        for h in range(GROUP):
            cols = slice(3 * HEAD * h, 3 * HEAD * h + 2 * HEAD)
            rest = slice(3 * HEAD * h + 2 * HEAD, 3 * HEAD * (h + 1))
            added = total[:, cols] + part[:, 2 * HEAD * h : 2 * HEAD * (h + 1)]
            outs[steps][0, :, cols] = added.astype(BF)
            outs[steps][0, :, rest] = total[:, rest].astype(BF)


def finish(place, nz, keep, got, low, high, near, far):
    rows = D // 8
    shape = (4, rows // nz, COLS)
    both = pl.BlockSpec((nz, 1) + shape[1:], lambda n, place: (0, n, 0, 0))
    part = pl.BlockSpec((rows, low.shape[1]), lambda n, place: (n, 0))
    fixed = pl.BlockSpec(near.shape, lambda n, place: (0, 0))
    return pl.pallas_call(
        lambda *refs: finish_kernel(nz, *refs),
        grid_spec=pltpu.PrefetchScalarGridSpec(
            num_scalar_prefetch=1,
            grid=(4,),
            in_specs=[both, both, part, part, fixed, fixed],
            out_specs=[pl.BlockSpec((1,) + shape[1:], lambda n, place: (n, 0, 0))] * nz,
            scratch_shapes=[pltpu.VMEM((rows, near.shape[1]), F32)],
        ),
        out_shape=[jax.ShapeDtypeStruct(shape, BF)] * nz,
        compiler_params=pltpu.CompilerParams(vmem_limit_bytes=60 * 1024 * 1024),
        cost_estimate=pl.CostEstimate(
            flops=FIRST, bytes_accessed=12 * 1024 * 1024, transcendentals=0
        ),
    )(place, keep, got, low, high, near, far)


def input_kernel(place_ref, dkv_ref, extra_ref, dq_ref, wkv_ref, wq_ref, *refs):
    step = pl.program_id(0)
    late = place_ref[step] >= 2
    extra = jnp.where(late, extra_ref[...].astype(F32), 0.0)
    dkv = (dkv_ref[...].astype(F32) + extra).astype(BF)
    total = dot(dkv, wkv_ref[...], 1, 1) + dot(dq_ref[...], wq_ref[...], 1, 1)
    half = total.shape[0] // 2
    if len(refs) == 2:
        refs[0][...] = total[:half].astype(BF)
        refs[1][...] = total[half:].astype(BF)
        return
    top_ref, low_ref, left_ref, right_ref, own_ref = refs

    @pl.when(step == 0)
    def _():
        left_ref[:half, :] = (total[:half] + top_ref[...].astype(F32)).astype(BF)
        left_ref[half:, :] = total[half:].astype(BF)

    @pl.when(step == 1)
    def _():
        right_ref[:half, :] = total[:half].astype(BF)
        right_ref[half:, :] = (total[half:] + low_ref[...].astype(F32)).astype(BF)

    @pl.when(step == 2)
    def _():
        own_ref[...] = total.astype(BF)


def input_grads(blocks, dkv, extra, dq, weight_kv, weight_q, back=()):
    wide = dq.shape[1]
    tok = dq.shape[0] // 4
    rows = lambda cols: pl.BlockSpec((tok, cols), lambda n, place: (place[n], 0))
    whole = lambda rows, cols: pl.BlockSpec((rows, cols), lambda n, place: (0, 0))
    made = [(tok, D)] * 3 if back else [(tok // 2, D)] * 2
    return pl.pallas_call(
        input_kernel,
        grid_spec=pltpu.PrefetchScalarGridSpec(
            num_scalar_prefetch=1,
            grid=(len(blocks),),
            in_specs=[
                rows(2 * wide),
                pl.BlockSpec((tok, 2 * wide), lambda n, place: (jnp.maximum(place[n] - 2, 0), 0)),
                rows(wide), whole(D, 2 * wide), whole(D, wide),
            ]
            + [whole(tok // 2, D)] * len(back),
            out_specs=[whole(*shape) for shape in made],
        ),
        out_shape=[jax.ShapeDtypeStruct(shape, BF) for shape in made],
        compiler_params=pltpu.CompilerParams(vmem_limit_bytes=60 * 1024 * 1024),
        cost_estimate=pl.CostEstimate(
            flops=FIRST, bytes_accessed=12 * 1024 * 1024, transcendentals=0
        ),
    )(jnp.stack(blocks), dkv, extra, dq, weight_kv, weight_q, *back)


def add_kernel(*refs):
    total = refs[0][...].astype(F32)
    for ref in refs[1:-1]:
        total = total + ref[...].astype(F32)
    refs[-1][...] = total.astype(BF)


def add_up(parts, weight):
    return pl.pallas_call(
        add_kernel,
        out_shape=jax.ShapeDtypeStruct(parts[0].shape, BF),
        compiler_params=pltpu.CompilerParams(vmem_limit_bytes=60 * 1024 * 1024),
        cost_estimate=pl.CostEstimate(
            flops=512 * weight, bytes_accessed=weight, transcendentals=0
        ),
    )(*parts)


def block_of(array, index, size):
    return lax.dynamic_slice_in_dim(array, index * size, size, 0)


def put(array, part, index):
    return lax.dynamic_update_slice_in_dim(array, part, index * part.shape[0], 0)


def on_device(sizes, inputs, w_query, w_key, w_value, out_grad):
    c = lax.axis_index("c")
    y = lax.axis_index("y")
    z = lax.axis_index("z")
    xl = lax.axis_index("xl")
    nz, nh = sizes["z"], sizes["xh"]
    tok = inputs.shape[1]
    half = tok // 2
    home = xl == c

    def ring(value, axis, steps, count=4):
        return lax.ppermute(value, axis, [(i, (i + steps) % count) for i in range(count)])

    def side_ring(value, axis, steps, count, own):
        pairs = []
        for side in range(2):
            core = side if own else 1 - side
            for i in range(count):
                j = (i + steps) % count
                pairs.append(((side * count + i) * 2 + core, (side * count + j) * 2 + core))
        return lax.ppermute(value, ("xl", axis, "c"), pairs)

    def swap_sides(value):
        return lax.ppermute(value, ("xl", "c"), [(1, 2), (2, 1)])

    at = lambda steps: (y + steps) % 4
    wide = GROUP * HEAD

    def crossed(value, steps):
        pairs = []
        for side in range(2):
            for i in range(4):
                for core in range(2):
                    there = ((core * 4 + (i + steps) % 4) * 2) + side
                    if steps or side != core:
                        pairs.append(((side * 4 + i) * 2 + core, there))
        return lax.ppermute(value, ("xl", "y", "c"), pairs)

    own = inputs[0]
    moved = swap_sides(own)
    left_home = side_ring(own, "y", 1, 4, True)
    right_home = side_ring(own, "y", -1, 4, True)
    weight_q, weight_kv = pick_weights(y, w_query, w_key, w_value)
    moved, left_home, right_home, weight_q, weight_kv, out_grad = lax.optimization_barrier(
        (moved, left_home, right_home, weight_q, weight_kv, out_grad)
    )
    left_away = side_ring(moved, "y", 1, 4, False)
    right_away = side_ring(moved, "y", -1, 4, False)
    cols = lambda index: lax.dynamic_slice_in_dim(out_grad[0], index * wide, wide, 1)
    dout_own = cols(y)
    dout_own = jnp.where(home, dout_own, crossed(dout_own, 0))
    dout_left = crossed(cols(at(1)), 1)
    dout_right = crossed(cols(at(-1)), -1)
    dout_far = crossed(cols(at(2)), 2)
    buffers = place_block((), own, moved, home, y, weight_kv, weight_q)
    dout_all = jnp.zeros((4 * tok, wide), BF)
    for part, index in ((dout_own, y), (dout_left, at(-1)), (dout_right, at(1)), (dout_far, at(2))):
        dout_all = put(dout_all, part, index)
    buffers, dout_all, left_away, right_away = lax.optimization_barrier(
        (buffers, dout_all, left_away, right_away)
    )
    far_top = jnp.where(home, left_home[:half], left_away[:half])
    far_low = jnp.where(home, right_home[half:], right_away[half:])
    far_top, far_low = lax.optimization_barrier((far_top, far_low))
    far_top = ring(far_top, "y", 1)
    far_low = ring(far_low, "y", -1)
    buffers = place_block(buffers, left_home, left_away, home, at(-1), weight_kv, weight_q)
    buffers = place_block(buffers, right_home, right_away, home, at(1), weight_kv, weight_q)
    tokens, kv, q = place_block(
        buffers, far_top, far_low, home, at(2), weight_kv, weight_q, split=True
    )

    halo = lax.ppermute(kv[2 * tok :], "c", [(0, 1)])
    bias = jnp.where(c == 0, -1e30, 0.0).astype(F32).reshape(1, 1)
    mine = jnp.stack([c, z])
    dq, dkv, dhalo, give, keep, low, high = attention(
        mine, bias, q, kv, halo, dout_all, tokens, nz
    )
    far_dhalo = lax.ppermute(dhalo, "c", [(1, 0)])
    got = lax.ppermute(give, "c", [(0, 1), (1, 0)])
    high = lax.ppermute(high, "c", [(0, 1)])
    far_parts = input_grads([at(2)], dkv, far_dhalo, dq, weight_kv, weight_q)
    back_top = ring(far_parts[0], "y", -1)
    back_low = ring(far_parts[1], "y", 1)
    keep, far_parts = lax.optimization_barrier((keep, far_parts))
    slabs = list(finish(mine, nz, keep, got, low, high, dhalo, far_dhalo))
    sent = [ring(slabs[steps], "z", steps, nz) for steps in range(1, nz)]
    dkv, slabs[0] = lax.optimization_barrier((dkv, slabs[0]))
    part_left, part_right, part_own = input_grads(
        [at(-1), at(1), y], dkv, far_dhalo, dq, weight_kv, weight_q, (back_top, back_low)
    )
    from_right = ring(part_left, "y", -1)
    from_left = ring(part_right, "y", 1)
    *sent, part_own = lax.optimization_barrier((*sent, part_own))
    share = add_up([slabs[0]] + sent, 4 * 1024 * 1024 * 1024)

    around = 2 * nh
    arrived = []
    for steps in range(1, around):
        pairs = []
        for core in range(2):
            for xh in range(nh):
                source = (xh * 2 + core + steps) % around
                pairs.append(
                    (((source % 2) * nh + source // 2) * 2 + core, (core * nh + xh) * 2 + core)
                )
        arrived.append(lax.ppermute(share, ("xl", "xh", "c"), pairs))
    *arrived, from_left, from_right = lax.optimization_barrier((*arrived, from_left, from_right))
    summed = share.astype(F32)
    for part in arrived:
        summed = summed + part.astype(F32)
    summed = summed.astype(BF)
    input_grad = part_own.astype(F32) + from_right.astype(F32) + from_left.astype(F32)
    input_grad = input_grad.astype(BF)
    away_grad = swap_sides(input_grad)

    fine = D // 8 // nz
    piece = lambda index: lax.dynamic_index_in_dim(summed, index % 4, 0, keepdims=False)
    gathered = jnp.zeros((3, fine, D), BF)

    def spread(gathered, piece, index):
        column = lambda i: piece[:, i * HEAD : (i + 1) * HEAD]
        parts = [[column(3 * h + part) for h in range(GROUP)] for part in (2, 0, 1)]
        parts = jnp.stack([jnp.concatenate(part, axis=1) for part in parts])
        return lax.dynamic_update_slice_in_dim(gathered, parts, index * wide, 2)

    gathered = spread(gathered, piece(y), y)
    for steps in range(1, 4):
        gathered = spread(gathered, side_ring(piece(y + steps), "y", steps, 4, True), at(-steps))
    result = jnp.zeros((3, nz * fine, D), BF)
    result = lax.dynamic_update_slice_in_dim(result, gathered, z * fine, 1)
    for steps in range(1, nz):
        result = lax.dynamic_update_slice_in_dim(
            result, side_ring(gathered, "z", steps, nz, True), (z - steps) % nz * fine, 1
        )
    result, away_grad = lax.optimization_barrier((result, away_grad))
    other = lax.ppermute(result, ("xl", "c"), [(0, 1), (3, 2)])
    input_grad = jnp.where(home, input_grad, away_grad)
    outs = [jnp.where(home, result[part], other[part]).astype(F32) for part in range(3)]
    return input_grad[None], outs[0], outs[1], outs[2]


def solution(mesh):
    dp = mesh.shape["dp"]
    nz = 4 if dp == 16 else 1
    nh = dp // 2 // nz
    sizes = {"xl": 2, "y": 4, "xh": nh, "z": nz, "c": 2}
    fine = Mesh(mesh.devices.reshape(tuple(sizes.values())), tuple(sizes))
    block, rollouts = ("xl", "y"), ("xh", "z", "c")
    placed = (P(rollouts, block, None), P(), P(), P(), P(rollouts, block, None))
    return jax.shard_map(
        lambda *arrays: on_device(sizes, *arrays),
        mesh=fine,
        in_specs=placed,
        out_specs=(P(rollouts, block, None), P(block, None), P(block, None), P(block, None)),
        check_vma=False,
    )
```

```python
import jax
import jax.numpy as jnp
from jax import lax
from jax.experimental import pallas as pl
from jax.experimental.pallas import tpu as pltpu
from jax.sharding import Mesh, PartitionSpec as P

D = 1536
HEADS = 12
HEAD = 128
GROUP = HEADS // 4
COLS = GROUP * 3 * HEAD
SCALE = HEAD ** (-0.5)
LOG2E = 1.4426950408889634
FIRST = 2**40
BF = jnp.bfloat16
F32 = jnp.float32


def dot(a, b, ca, cb):
    return lax.dot_general(a, b, (((ca,), (cb,)), ((), ())), preferred_element_type=F32)


def attention_kernel(
    tok, nz, place_ref, bias_ref, q_ref, kv_ref, halo_ref, dout_ref, turned_ref,
    dq_ref, dkv_ref, dhalo_ref, give_ref, keep_ref, low_ref, high_ref,
    acc_ref, held_ref, grad_ref, sem_ref,
):
    step = pl.program_id(0)
    fetch = pltpu.make_async_copy(turned_ref, held_ref, sem_ref)

    @pl.when(step == 0)
    def _():
        fetch.start()

    bias = bias_ref[0, 0]
    zero = jnp.zeros((tok, HEAD), BF)

    def first(i):
        here = slice(i * tok, (i + 1) * tok)
        kv = kv_ref[max(i - 2, 0) * tok : (i + 1) * tok, :]
        if i < 2:
            kv = jnp.concatenate([halo_ref[i * tok : 2 * tok, :], kv], axis=0)
        qd = jnp.concatenate(
            [
                jnp.concatenate([q_ref[here, :], zero], axis=1),
                jnp.concatenate([zero, dout_ref[here, :]], axis=1),
            ],
            axis=0,
        )
        return kv, qd, dot(kv, qd, 1, 1)

    def second(i, kv, qd, both):
        s = both[:, :tok]
        dp = both[:, tok:]
        if i < 2:
            edge = (2 - i) * tok
            s = jnp.concatenate([s[:edge] + bias, s[edge:]], axis=0)
        peak = jnp.max(s, axis=0, keepdims=True) * (SCALE * LOG2E)
        e = jnp.exp2(s * (SCALE * LOG2E) - peak)
        p = e * (1.0 / jnp.sum(e, axis=0, keepdims=True))
        delta = jnp.sum(p * dp, axis=0, keepdims=True)
        ds = (p * (dp - delta)).astype(BF)
        dkv = dot(jnp.concatenate([ds, p.astype(BF)], axis=1), qd, 1, 0)
        for j in range(3):
            rows = slice((i + j) * tok, (i + j + 1) * tok)
            part = dkv[j * tok : (j + 1) * tok]
            if i == 0 or j == 2:
                acc_ref[rows, :] = part
            else:
                acc_ref[rows, :] += part
        dq = dot(kv[:, :HEAD], ds, 0, 0).T * SCALE
        dq_ref[i * tok : (i + 1) * tok, :] = dq.astype(BF)

    ahead = first(0)
    for i in range(4):
        now = ahead
        if i < 3:
            ahead = first(i + 1)
        second(i, *now)
    dkv_ref[:, :HEAD] = (acc_ref[2 * tok :, :HEAD] * SCALE).astype(BF)
    dkv_ref[:, HEAD:] = acc_ref[2 * tok :, HEAD:].astype(BF)
    dhalo_ref[:, :HEAD] = (acc_ref[: 2 * tok, :HEAD] * SCALE).astype(BF)
    dhalo_ref[:, HEAD:] = acc_ref[: 2 * tok, HEAD:].astype(BF)

    @pl.when(step == 0)
    def _():
        fetch.wait()
        low_ref[...] = held_ref[: D // 2, 2 * tok :]
        high_ref[...] = held_ref[D // 2 :, 2 * tok :]

    grad_ref[:, : 2 * HEAD] = dot(held_ref[...], dkv_ref[...], 1, 0)
    grad_ref[:, 2 * HEAD :] = dot(held_ref[...], dq_ref[...], 1, 0)
    fine = D // 8 // nz
    for out_ref, side in ((give_ref, 1 - place_ref[0]), (keep_ref, place_ref[0])):
        for steps in range(nz):
            for y in range(4):
                start = side * (D // 2) + (y * nz + lax.rem(place_ref[1] + steps, nz)) * fine
                rows = pl.ds(pl.multiple_of(start, 16), fine)
                out_ref[steps, y] = grad_ref[rows, :].astype(BF)


def attention(place, bias, q, kv, halo, dout, turned, nz):
    tok = q.shape[0] // 4
    one = pl.BlockSpec((4 * tok, HEAD), lambda h, place: (0, h))
    two = pl.BlockSpec((4 * tok, 2 * HEAD), lambda h, place: (0, h))
    edge = pl.BlockSpec((2 * tok, 2 * HEAD), lambda h, place: (0, h))
    corner = pl.BlockSpec((D // 2, 2 * tok), lambda h, place: (0, 0))
    shape = (nz, 4, D // 8 // nz, COLS)
    slabs = pl.BlockSpec(shape[:3] + (3 * HEAD,), lambda h, place: (0, 0, 0, h))
    made = lambda shape: jax.ShapeDtypeStruct(shape, BF)
    return pl.pallas_call(
        lambda *refs: attention_kernel(tok, nz, *refs),
        grid_spec=pltpu.PrefetchScalarGridSpec(
            num_scalar_prefetch=1,
            grid=(GROUP,),
            in_specs=[
                pl.BlockSpec(memory_space=pltpu.SMEM), one, two, edge, one,
                pl.BlockSpec(memory_space=pl.ANY),
            ],
            out_specs=[one, two, edge, slabs, slabs, corner, corner],
            scratch_shapes=[
                pltpu.VMEM((6 * tok, 2 * HEAD), F32),
                pltpu.VMEM((D, 4 * tok), BF),
                pltpu.VMEM((D, 3 * HEAD), F32),
                pltpu.SemaphoreType.DMA,
            ],
        ),
        out_shape=[
            made(q.shape), made(kv.shape), made(halo.shape), made(shape), made(shape),
            made((D // 2, 2 * tok)), made((D // 2, 2 * tok)),
        ],
        compiler_params=pltpu.CompilerParams(vmem_limit_bytes=60 * 1024 * 1024),
        cost_estimate=pl.CostEstimate(
            flops=2 * 5 * 4 * GROUP * 3 * tok * tok * HEAD * 2 + 8 * tok * D * COLS,
            bytes_accessed=24 * kv.size,
            transcendentals=4 * GROUP * 3 * tok * tok,
        ),
    )(place, bias, q, kv, halo, dout, turned)


def pick_kernel(place_ref, query_ref, key_ref, value_ref, q_ref, kv_ref):
    q_ref[...] = query_ref[...]
    kv_ref[:, :HEAD] = key_ref[...]
    kv_ref[:, HEAD:] = value_ref[...]


def pick_weights(index, w_query, w_key, w_value):
    piece = pl.BlockSpec((D, HEAD), lambda h, place: (0, place[0] * GROUP + h))
    return pl.pallas_call(
        pick_kernel,
        grid_spec=pltpu.PrefetchScalarGridSpec(
            num_scalar_prefetch=1,
            grid=(GROUP,),
            in_specs=[piece, piece, piece],
            out_specs=[
                pl.BlockSpec((D, HEAD), lambda h, place: (0, h)),
                pl.BlockSpec((D, 2 * HEAD), lambda h, place: (0, h)),
            ],
        ),
        out_shape=[
            jax.ShapeDtypeStruct((D, GROUP * HEAD), BF),
            jax.ShapeDtypeStruct((D, 2 * GROUP * HEAD), BF),
        ],
        compiler_params=pltpu.CompilerParams(vmem_limit_bytes=60 * 1024 * 1024),
        cost_estimate=pl.CostEstimate(
            flops=FIRST, bytes_accessed=4 * D * COLS, transcendentals=0
        ),
    )(index.reshape(1), w_query, w_key, w_value)


def choose_kernel(place_ref, left_home, left_away, right_home, right_away, top_ref, low_ref):
    @pl.when(place_ref[0] == 1)
    def _():
        top_ref[...] = left_home[...]
        low_ref[...] = right_home[...]

    @pl.when(place_ref[0] == 0)
    def _():
        top_ref[...] = left_away[...]
        low_ref[...] = right_away[...]


def choose(home, left_home, left_away, right_home, right_away):
    half = left_home.shape[0] // 2
    part = lambda side: pl.BlockSpec((half, D // 2), lambda n, place: (side, n))
    return pl.pallas_call(
        choose_kernel,
        grid_spec=pltpu.PrefetchScalarGridSpec(
            num_scalar_prefetch=1,
            grid=(2,),
            in_specs=[part(0), part(0), part(1), part(1)],
            out_specs=[part(0), part(0)],
        ),
        out_shape=[jax.ShapeDtypeStruct((half, D), BF)] * 2,
        compiler_params=pltpu.CompilerParams(vmem_limit_bytes=60 * 1024 * 1024),
        cost_estimate=pl.CostEstimate(
            flops=half * D, bytes_accessed=12 * half * D, transcendentals=0
        ),
    )(home.astype(jnp.int32).reshape(1), left_home, left_away, right_home, right_away)


def place_kernel(split, place_ref, a_ref, b_ref, wkv_ref, wq_ref, *refs):
    t_ref, kv_ref, q_ref, block_ref = refs[-4:]
    step = pl.program_id(0)

    @pl.when(step == 0)
    def _():
        if split:
            half = a_ref.shape[0]
            block_ref[:half, :] = a_ref[...]
            block_ref[half:, :] = b_ref[...]
        else:
            block_ref[...] = a_ref[...]

            @pl.when(place_ref[1] == 0)
            def _():
                block_ref[...] = b_ref[...]

    block = block_ref[...]
    kv_ref[...] = dot(block, wkv_ref[...], 1, 0).astype(BF)
    q_ref[...] = dot(block, wq_ref[...], 1, 0).astype(BF)
    third = D // GROUP
    t_ref[...] = block_ref[:, pl.ds(pl.multiple_of(step * third, 128), third)].T


def place_block(buffers, a, b, home, index, weight_kv, weight_q, split=False):
    tok = a.shape[0] * (2 if split else 1)
    shapes = ((D, 4 * tok), (4 * tok, 2 * GROUP * HEAD), (4 * tok, GROUP * HEAD))
    whole = pl.BlockSpec(a.shape, lambda h, place: (0, 0))
    anywhere = pl.BlockSpec(memory_space=pl.ANY)
    return pl.pallas_call(
        lambda *refs: place_kernel(split, *refs),
        grid_spec=pltpu.PrefetchScalarGridSpec(
            num_scalar_prefetch=1,
            grid=(GROUP,),
            in_specs=[
                whole, whole,
                pl.BlockSpec((D, 2 * HEAD), lambda h, place: (0, h)),
                pl.BlockSpec((D, HEAD), lambda h, place: (0, h)),
            ]
            + [anywhere] * len(buffers),
            out_specs=[
                pl.BlockSpec((D // GROUP, tok), lambda h, place: (h, place[0])),
                pl.BlockSpec((tok, 2 * HEAD), lambda h, place: (place[0], h)),
                pl.BlockSpec((tok, HEAD), lambda h, place: (place[0], h)),
            ],
            scratch_shapes=[pltpu.VMEM((tok, D), BF)],
        ),
        out_shape=[jax.ShapeDtypeStruct(shape, BF) for shape in shapes],
        input_output_aliases={5: 0, 6: 1, 7: 2} if buffers else {},
        compiler_params=pltpu.CompilerParams(vmem_limit_bytes=60 * 1024 * 1024),
        cost_estimate=pl.CostEstimate(
            flops=FIRST, bytes_accessed=8 * tok * D, transcendentals=0
        ),
    )(jnp.stack([index, home.astype(jnp.int32)]), a, b, weight_kv, weight_q, *buffers)


def finish_kernel(nz, place_ref, keep_ref, got_ref, low_ref, high_ref, near_ref, far_ref, *refs):
    outs, acc_ref = refs[:-1], refs[-1]
    first = place_ref[0] == 0

    @pl.when(first)
    def _():
        acc_ref[...] = dot(low_ref[...], far_ref[...], 1, 0)

    @pl.when(jnp.logical_not(first))
    def _():
        acc_ref[...] = dot(high_ref[...], near_ref[...], 1, 0)

    fine = acc_ref.shape[0] // nz
    for steps in range(nz):
        at = pl.multiple_of(lax.rem(place_ref[1] + steps, nz) * fine, 16)
        total = keep_ref[steps, 0].astype(F32) + got_ref[steps, 0].astype(F32)
        part = acc_ref[pl.ds(at, fine), :]
        for h in range(GROUP):
            cols = slice(3 * HEAD * h, 3 * HEAD * h + 2 * HEAD)
            rest = slice(3 * HEAD * h + 2 * HEAD, 3 * HEAD * (h + 1))
            added = total[:, cols] + part[:, 2 * HEAD * h : 2 * HEAD * (h + 1)]
            outs[steps][0, :, cols] = added.astype(BF)
            outs[steps][0, :, rest] = total[:, rest].astype(BF)


def finish(place, nz, keep, got, low, high, near, far):
    rows = D // 8
    shape = (4, rows // nz, COLS)
    both = pl.BlockSpec((nz, 1) + shape[1:], lambda n, place: (0, n, 0, 0))
    part = pl.BlockSpec((rows, low.shape[1]), lambda n, place: (n, 0))
    fixed = pl.BlockSpec(near.shape, lambda n, place: (0, 0))
    return pl.pallas_call(
        lambda *refs: finish_kernel(nz, *refs),
        grid_spec=pltpu.PrefetchScalarGridSpec(
            num_scalar_prefetch=1,
            grid=(4,),
            in_specs=[both, both, part, part, fixed, fixed],
            out_specs=[pl.BlockSpec((1,) + shape[1:], lambda n, place: (n, 0, 0))] * nz,
            scratch_shapes=[pltpu.VMEM((rows, near.shape[1]), F32)],
        ),
        out_shape=[jax.ShapeDtypeStruct(shape, BF)] * nz,
        compiler_params=pltpu.CompilerParams(vmem_limit_bytes=60 * 1024 * 1024),
        cost_estimate=pl.CostEstimate(
            flops=FIRST, bytes_accessed=12 * 1024 * 1024, transcendentals=0
        ),
    )(place, keep, got, low, high, near, far)


def input_kernel(place_ref, dkv_ref, extra_ref, dq_ref, wkv_ref, wq_ref, *refs):
    step = pl.program_id(0)
    late = place_ref[step] >= 2
    extra = jnp.where(late, extra_ref[...].astype(F32), 0.0)
    dkv = (dkv_ref[...].astype(F32) + extra).astype(BF)
    total = dot(dkv, wkv_ref[...], 1, 1) + dot(dq_ref[...], wq_ref[...], 1, 1)
    half = total.shape[0] // 2
    if len(refs) == 1:
        refs[0][...] = total.astype(BF)
        return
    if len(refs) == 2:
        refs[0][...] = total[:half].astype(BF)
        refs[1][...] = total[half:].astype(BF)
        return
    top_ref, low_ref, left_ref, right_ref = refs

    @pl.when(step == 0)
    def _():
        left_ref[:half, :] = (total[:half] + top_ref[...].astype(F32)).astype(BF)
        left_ref[half:, :] = total[half:].astype(BF)

    @pl.when(step == 1)
    def _():
        right_ref[:half, :] = total[:half].astype(BF)
        right_ref[half:, :] = (total[half:] + low_ref[...].astype(F32)).astype(BF)


def input_grads(blocks, dkv, extra, dq, weight_kv, weight_q, heights, work, back=()):
    wide = dq.shape[1]
    tok = dq.shape[0] // 4
    rows = lambda cols: pl.BlockSpec((tok, cols), lambda n, place: (place[n], 0))
    whole = lambda rows, cols: pl.BlockSpec((rows, cols), lambda n, place: (0, 0))
    made = [(height, D) for height in heights]
    return pl.pallas_call(
        input_kernel,
        grid_spec=pltpu.PrefetchScalarGridSpec(
            num_scalar_prefetch=1,
            grid=(len(blocks),),
            in_specs=[
                rows(2 * wide),
                pl.BlockSpec((tok, 2 * wide), lambda n, place: (jnp.maximum(place[n] - 2, 0), 0)),
                rows(wide), whole(D, 2 * wide), whole(D, wide),
            ]
            + [whole(tok // 2, D)] * len(back),
            out_specs=[whole(*shape) for shape in made],
        ),
        out_shape=[jax.ShapeDtypeStruct(shape, BF) for shape in made],
        compiler_params=pltpu.CompilerParams(vmem_limit_bytes=60 * 1024 * 1024),
        cost_estimate=pl.CostEstimate(
            flops=work, bytes_accessed=12 * 1024 * 1024, transcendentals=0
        ),
    )(jnp.stack(blocks), dkv, extra, dq, weight_kv, weight_q, *back)


def block_of(array, index, size):
    return lax.dynamic_slice_in_dim(array, index * size, size, 0)


def put(array, part, index):
    return lax.dynamic_update_slice_in_dim(array, part, index * part.shape[0], 0)


def on_device(sizes, inputs, w_query, w_key, w_value, out_grad):
    c = lax.axis_index("c")
    y = lax.axis_index("y")
    z = lax.axis_index("z")
    xl = lax.axis_index("xl")
    nz, nh = sizes["z"], sizes["xh"]
    tok = inputs.shape[1]
    half = tok // 2
    home = xl == c

    def ring(value, axis, steps, count=4):
        return lax.ppermute(value, axis, [(i, (i + steps) % count) for i in range(count)])

    def side_ring(value, axis, steps, count, own):
        pairs = []
        for side in range(2):
            core = side if own else 1 - side
            for i in range(count):
                j = (i + steps) % count
                pairs.append(((side * count + i) * 2 + core, (side * count + j) * 2 + core))
        return lax.ppermute(value, ("xl", axis, "c"), pairs)

    def swap_sides(value):
        return lax.ppermute(value, ("xl", "c"), [(1, 2), (2, 1)])

    at = lambda steps: (y + steps) % 4
    wide = GROUP * HEAD

    def crossed(value, steps):
        pairs = []
        for side in range(2):
            for i in range(4):
                for core in range(2):
                    there = ((core * 4 + (i + steps) % 4) * 2) + side
                    if steps or side != core:
                        pairs.append(((side * 4 + i) * 2 + core, there))
        return lax.ppermute(value, ("xl", "y", "c"), pairs)

    own = inputs[0]
    moved = swap_sides(own)
    left_home = side_ring(own, "y", 1, 4, True)
    right_home = side_ring(own, "y", -1, 4, True)
    weight_q, weight_kv = pick_weights(y, w_query, w_key, w_value)
    moved, left_home, right_home, weight_q, weight_kv, out_grad = lax.optimization_barrier(
        (moved, left_home, right_home, weight_q, weight_kv, out_grad)
    )
    left_away = side_ring(moved, "y", 1, 4, False)
    right_away = side_ring(moved, "y", -1, 4, False)
    cols = lambda index: lax.dynamic_slice_in_dim(out_grad[0], index * wide, wide, 1)
    dout_own = cols(y)
    dout_own = jnp.where(home, dout_own, crossed(dout_own, 0))
    dout_left = crossed(cols(at(1)), 1)
    dout_right = crossed(cols(at(-1)), -1)
    dout_far = crossed(cols(at(2)), 2)
    buffers = place_block((), own, moved, home, y, weight_kv, weight_q)
    dout_all = jnp.zeros((4 * tok, wide), BF)
    for part, index in ((dout_far, at(2)), (dout_left, at(-1)), (dout_right, at(1)), (dout_own, y)):
        dout_all = put(dout_all, part, index)
    buffers, dout_all, left_away, right_away = lax.optimization_barrier(
        (buffers, dout_all, left_away, right_away)
    )
    far_top, far_low = choose(home, left_home, left_away, right_home, right_away)
    far_top = ring(far_top, "y", 1)
    far_low = ring(far_low, "y", -1)
    buffers = place_block(buffers, left_home, left_away, home, at(-1), weight_kv, weight_q)
    buffers = place_block(buffers, right_home, right_away, home, at(1), weight_kv, weight_q)
    tokens, kv, q = place_block(
        buffers, far_top, far_low, home, at(2), weight_kv, weight_q, split=True
    )

    halo = lax.ppermute(kv[2 * tok :], "c", [(0, 1)])
    bias = jnp.where(c == 0, -1e30, 0.0).astype(F32).reshape(1, 1)
    mine = jnp.stack([c, z])
    dq, dkv, dhalo, give, keep, low, high = attention(
        mine, bias, q, kv, halo, dout_all, tokens, nz
    )
    far_dhalo = lax.ppermute(dhalo, "c", [(1, 0)])
    got = lax.ppermute(give, "c", [(0, 1), (1, 0)])
    high = lax.ppermute(high, "c", [(0, 1)])
    far_parts = input_grads(
        [at(2)], dkv, far_dhalo, dq, weight_kv, weight_q, (half, half), FIRST
    )
    back_top = ring(far_parts[0], "y", -1)
    back_low = ring(far_parts[1], "y", 1)
    keep, far_parts = lax.optimization_barrier((keep, far_parts))
    slabs = list(finish(mine, nz, keep, got, low, high, dhalo, far_dhalo))
    sent = [ring(slabs[steps], "z", steps, nz) for steps in range(1, nz)]
    dkv, slabs[0] = lax.optimization_barrier((dkv, slabs[0]))
    part_left, part_right = input_grads(
        [at(-1), at(1)], dkv, far_dhalo, dq, weight_kv, weight_q, (tok, tok), FIRST,
        (back_top, back_low),
    )
    from_right = ring(part_left, "y", -1)
    from_left = ring(part_right, "y", 1)
    *sent, part_left = lax.optimization_barrier((*sent, part_left))
    share = slabs[0].astype(F32)
    for part in sent:
        share = share + part.astype(F32)
    share = share.astype(BF)

    dkv, share = lax.optimization_barrier((dkv, share))
    (part_own,) = input_grads(
        [y], dkv, far_dhalo, dq, weight_kv, weight_q, (tok,), 2 * tok * D * COLS
    )
    around = 2 * nh
    arrived = []
    for steps in range(1, around):
        pairs = []
        for core in range(2):
            for xh in range(nh):
                source = (xh * 2 + core + steps) % around
                pairs.append(
                    (((source % 2) * nh + source // 2) * 2 + core, (core * nh + xh) * 2 + core)
                )
        arrived.append(lax.ppermute(share, ("xl", "xh", "c"), pairs))
    *arrived, from_left, from_right = lax.optimization_barrier((*arrived, from_left, from_right))
    summed = share.astype(F32)
    for part in arrived:
        summed = summed + part.astype(F32)
    summed = summed.astype(BF)
    input_grad = part_own.astype(F32) + from_right.astype(F32) + from_left.astype(F32)
    input_grad = input_grad.astype(BF)
    away_grad = swap_sides(input_grad)

    fine = D // 8 // nz
    piece = lambda index: lax.dynamic_index_in_dim(summed, index % 4, 0, keepdims=False)
    gathered = jnp.zeros((3, fine, D), BF)

    def spread(gathered, piece, index):
        column = lambda i: piece[:, i * HEAD : (i + 1) * HEAD]
        parts = [[column(3 * h + part) for h in range(GROUP)] for part in (2, 0, 1)]
        parts = jnp.stack([jnp.concatenate(part, axis=1) for part in parts])
        return lax.dynamic_update_slice_in_dim(gathered, parts, index * wide, 2)

    gathered = spread(gathered, piece(y), y)
    for steps in range(1, 4):
        gathered = spread(gathered, side_ring(piece(y + steps), "y", steps, 4, True), at(-steps))
    result = jnp.zeros((3, nz * fine, D), BF)
    result = lax.dynamic_update_slice_in_dim(result, gathered, z * fine, 1)
    for steps in range(1, nz):
        result = lax.dynamic_update_slice_in_dim(
            result, side_ring(gathered, "z", steps, nz, True), (z - steps) % nz * fine, 1
        )
    result, away_grad = lax.optimization_barrier((result, away_grad))
    other = lax.ppermute(result, ("xl", "c"), [(0, 1), (3, 2)])
    input_grad = jnp.where(home, input_grad, away_grad)
    outs = [jnp.where(home, result[part], other[part]).astype(F32) for part in range(3)]
    return input_grad[None], outs[0], outs[1], outs[2]


def solution(mesh):
    dp = mesh.shape["dp"]
    nz = 4 if dp == 16 else 1
    nh = dp // 2 // nz
    sizes = {"xl": 2, "y": 4, "xh": nh, "z": nz, "c": 2}
    fine = Mesh(mesh.devices.reshape(tuple(sizes.values())), tuple(sizes))
    block, rollouts = ("xl", "y"), ("xh", "z", "c")
    placed = (P(rollouts, block, None), P(), P(), P(), P(rollouts, block, None))
    return jax.shard_map(
        lambda *arrays: on_device(sizes, *arrays),
        mesh=fine,
        in_specs=placed,
        out_specs=(P(rollouts, block, None), P(block, None), P(block, None), P(block, None)),
        check_vma=False,
    )
```

```python
import jax
import jax.numpy as jnp
from jax import lax
from jax.experimental import pallas as pl
from jax.experimental.pallas import tpu as pltpu
from jax.sharding import Mesh, PartitionSpec as P

D = 1536
HEADS = 12
HEAD = 128
GROUP = HEADS // 4
COLS = GROUP * 3 * HEAD
SCALE = HEAD ** (-0.5)
LOG2E = 1.4426950408889634
FIRST = 2**40
BF = jnp.bfloat16
F32 = jnp.float32


def dot(a, b, ca, cb):
    return lax.dot_general(a, b, (((ca,), (cb,)), ((), ())), preferred_element_type=F32)


def attention_kernel(
    tok, nz, place_ref, bias_ref, q_ref, kv_ref, halo_ref, dout_ref, turned_ref,
    dq_ref, dkv_ref, dhalo_ref, give_ref, keep_ref, low_ref, high_ref,
    acc_ref, held_ref, grad_ref, sem_ref,
):
    step = pl.program_id(0)
    fetch = pltpu.make_async_copy(turned_ref, held_ref, sem_ref)

    @pl.when(step == 0)
    def _():
        fetch.start()

    bias = bias_ref[0, 0]
    zero = jnp.zeros((tok, HEAD), BF)

    def first(i):
        here = slice(i * tok, (i + 1) * tok)
        kv = kv_ref[max(i - 2, 0) * tok : (i + 1) * tok, :]
        if i < 2:
            kv = jnp.concatenate([halo_ref[i * tok : 2 * tok, :], kv], axis=0)
        qd = jnp.concatenate(
            [
                jnp.concatenate([q_ref[here, :], zero], axis=1),
                jnp.concatenate([zero, dout_ref[here, :]], axis=1),
            ],
            axis=0,
        )
        return kv, qd, dot(kv, qd, 1, 1)

    def second(i, kv, qd, both):
        s = both[:, :tok]
        dp = both[:, tok:]
        if i < 2:
            edge = (2 - i) * tok
            s = jnp.concatenate([s[:edge] + bias, s[edge:]], axis=0)
        peak = jnp.max(s, axis=0, keepdims=True) * (SCALE * LOG2E)
        e = jnp.exp2(s * (SCALE * LOG2E) - peak)
        p = e * (1.0 / jnp.sum(e, axis=0, keepdims=True))
        delta = jnp.sum(p * dp, axis=0, keepdims=True)
        ds = (p * (dp - delta)).astype(BF)
        sides = jnp.concatenate([ds, p.astype(BF)], axis=1)
        for j in range(3):
            rows = slice((i + j) * tok, (i + j + 1) * tok)
            part = dot(sides[j * tok : (j + 1) * tok], qd, 1, 0)
            if i == 0 or j == 2:
                acc_ref[rows, :] = part
            else:
                acc_ref[rows, :] += part
        dq = dot(kv[:, :HEAD], ds, 0, 0).T * SCALE
        dq_ref[i * tok : (i + 1) * tok, :] = dq.astype(BF)

    ahead = first(0)
    for i in range(4):
        now = ahead
        if i < 3:
            ahead = first(i + 1)
        second(i, *now)
    dkv_ref[:, :HEAD] = (acc_ref[2 * tok :, :HEAD] * SCALE).astype(BF)
    dkv_ref[:, HEAD:] = acc_ref[2 * tok :, HEAD:].astype(BF)
    dhalo_ref[:, :HEAD] = (acc_ref[: 2 * tok, :HEAD] * SCALE).astype(BF)
    dhalo_ref[:, HEAD:] = acc_ref[: 2 * tok, HEAD:].astype(BF)

    @pl.when(step == 0)
    def _():
        fetch.wait()
        low_ref[...] = held_ref[: D // 2, 2 * tok :]
        high_ref[...] = held_ref[D // 2 :, 2 * tok :]

    both = jnp.concatenate([dkv_ref[...], dq_ref[...]], axis=1)
    for m in range(8):
        part = slice(m * D // 8, (m + 1) * D // 8)
        grad_ref[part, :] = dot(held_ref[part, :], both, 1, 0)
    fine = D // 8 // nz
    for out_ref, side in ((give_ref, 1 - place_ref[0]), (keep_ref, place_ref[0])):
        for steps in range(nz):
            for y in range(4):
                start = side * (D // 2) + (y * nz + lax.rem(place_ref[1] + steps, nz)) * fine
                rows = pl.ds(pl.multiple_of(start, 16), fine)
                out_ref[steps, y] = grad_ref[rows, :].astype(BF)


def attention(place, bias, q, kv, halo, dout, turned, nz):
    tok = q.shape[0] // 4
    one = pl.BlockSpec((4 * tok, HEAD), lambda h, place: (0, h))
    two = pl.BlockSpec((4 * tok, 2 * HEAD), lambda h, place: (0, h))
    edge = pl.BlockSpec((2 * tok, 2 * HEAD), lambda h, place: (0, h))
    corner = pl.BlockSpec((D // 2, 2 * tok), lambda h, place: (0, 0))
    shape = (nz, 4, D // 8 // nz, COLS)
    slabs = pl.BlockSpec(shape[:3] + (3 * HEAD,), lambda h, place: (0, 0, 0, h))
    made = lambda shape: jax.ShapeDtypeStruct(shape, BF)
    return pl.pallas_call(
        lambda *refs: attention_kernel(tok, nz, *refs),
        grid_spec=pltpu.PrefetchScalarGridSpec(
            num_scalar_prefetch=1,
            grid=(GROUP,),
            in_specs=[
                pl.BlockSpec(memory_space=pltpu.SMEM), one, two, edge, one,
                pl.BlockSpec(memory_space=pl.ANY),
            ],
            out_specs=[one, two, edge, slabs, slabs, corner, corner],
            scratch_shapes=[
                pltpu.VMEM((6 * tok, 2 * HEAD), F32),
                pltpu.VMEM((D, 4 * tok), BF),
                pltpu.VMEM((D, 3 * HEAD), F32),
                pltpu.SemaphoreType.DMA,
            ],
        ),
        out_shape=[
            made(q.shape), made(kv.shape), made(halo.shape), made(shape), made(shape),
            made((D // 2, 2 * tok)), made((D // 2, 2 * tok)),
        ],
        compiler_params=pltpu.CompilerParams(vmem_limit_bytes=60 * 1024 * 1024),
        cost_estimate=pl.CostEstimate(
            flops=2 * 5 * 4 * GROUP * 3 * tok * tok * HEAD * 2 + 8 * tok * D * COLS,
            bytes_accessed=24 * kv.size,
            transcendentals=4 * GROUP * 3 * tok * tok,
        ),
    )(place, bias, q, kv, halo, dout, turned)


def pick_kernel(place_ref, query_ref, key_ref, value_ref, q_ref, kv_ref):
    q_ref[...] = query_ref[...]
    kv_ref[:, :HEAD] = key_ref[...]
    kv_ref[:, HEAD:] = value_ref[...]


def pick_weights(index, w_query, w_key, w_value):
    piece = pl.BlockSpec((D, HEAD), lambda h, place: (0, place[0] * GROUP + h))
    return pl.pallas_call(
        pick_kernel,
        grid_spec=pltpu.PrefetchScalarGridSpec(
            num_scalar_prefetch=1,
            grid=(GROUP,),
            in_specs=[piece, piece, piece],
            out_specs=[
                pl.BlockSpec((D, HEAD), lambda h, place: (0, h)),
                pl.BlockSpec((D, 2 * HEAD), lambda h, place: (0, h)),
            ],
        ),
        out_shape=[
            jax.ShapeDtypeStruct((D, GROUP * HEAD), BF),
            jax.ShapeDtypeStruct((D, 2 * GROUP * HEAD), BF),
        ],
        compiler_params=pltpu.CompilerParams(vmem_limit_bytes=60 * 1024 * 1024),
        cost_estimate=pl.CostEstimate(
            flops=FIRST, bytes_accessed=4 * D * COLS, transcendentals=0
        ),
    )(index.reshape(1), w_query, w_key, w_value)


def choose_kernel(place_ref, left_home, left_away, right_home, right_away, top_ref, low_ref):
    @pl.when(place_ref[0] == 1)
    def _():
        top_ref[...] = left_home[...]
        low_ref[...] = right_home[...]

    @pl.when(place_ref[0] == 0)
    def _():
        top_ref[...] = left_away[...]
        low_ref[...] = right_away[...]


def choose(home, left_home, left_away, right_home, right_away):
    half = left_home.shape[0] // 2
    part = lambda side: pl.BlockSpec((half, D // 2), lambda n, place: (side, n))
    return pl.pallas_call(
        choose_kernel,
        grid_spec=pltpu.PrefetchScalarGridSpec(
            num_scalar_prefetch=1,
            grid=(2,),
            in_specs=[part(0), part(0), part(1), part(1)],
            out_specs=[part(0), part(0)],
        ),
        out_shape=[jax.ShapeDtypeStruct((half, D), BF)] * 2,
        compiler_params=pltpu.CompilerParams(vmem_limit_bytes=60 * 1024 * 1024),
        cost_estimate=pl.CostEstimate(
            flops=half * D, bytes_accessed=12 * half * D, transcendentals=0
        ),
    )(home.astype(jnp.int32).reshape(1), left_home, left_away, right_home, right_away)


def place_kernel(split, place_ref, a_ref, b_ref, wkv_ref, wq_ref, *refs):
    t_ref, kv_ref, q_ref, block_ref = refs[-4:]
    step = pl.program_id(0)

    @pl.when(step == 0)
    def _():
        if split:
            half = a_ref.shape[0]
            block_ref[:half, :] = a_ref[...]
            block_ref[half:, :] = b_ref[...]
        else:
            block_ref[...] = a_ref[...]

            @pl.when(place_ref[1] == 0)
            def _():
                block_ref[...] = b_ref[...]

    block = block_ref[...]
    kv_ref[...] = dot(block, wkv_ref[...], 1, 0).astype(BF)
    q_ref[...] = dot(block, wq_ref[...], 1, 0).astype(BF)
    third = D // GROUP
    t_ref[...] = block_ref[:, pl.ds(pl.multiple_of(step * third, 128), third)].T


def place_block(buffers, a, b, home, index, weight_kv, weight_q, split=False):
    tok = a.shape[0] * (2 if split else 1)
    shapes = ((D, 4 * tok), (4 * tok, 2 * GROUP * HEAD), (4 * tok, GROUP * HEAD))
    whole = pl.BlockSpec(a.shape, lambda h, place: (0, 0))
    anywhere = pl.BlockSpec(memory_space=pl.ANY)
    return pl.pallas_call(
        lambda *refs: place_kernel(split, *refs),
        grid_spec=pltpu.PrefetchScalarGridSpec(
            num_scalar_prefetch=1,
            grid=(GROUP,),
            in_specs=[
                whole, whole,
                pl.BlockSpec((D, 2 * HEAD), lambda h, place: (0, h)),
                pl.BlockSpec((D, HEAD), lambda h, place: (0, h)),
            ]
            + [anywhere] * len(buffers),
            out_specs=[
                pl.BlockSpec((D // GROUP, tok), lambda h, place: (h, place[0])),
                pl.BlockSpec((tok, 2 * HEAD), lambda h, place: (place[0], h)),
                pl.BlockSpec((tok, HEAD), lambda h, place: (place[0], h)),
            ],
            scratch_shapes=[pltpu.VMEM((tok, D), BF)],
        ),
        out_shape=[jax.ShapeDtypeStruct(shape, BF) for shape in shapes],
        input_output_aliases={5: 0, 6: 1, 7: 2} if buffers else {},
        compiler_params=pltpu.CompilerParams(vmem_limit_bytes=60 * 1024 * 1024),
        cost_estimate=pl.CostEstimate(
            flops=FIRST, bytes_accessed=8 * tok * D, transcendentals=0
        ),
    )(jnp.stack([index, home.astype(jnp.int32)]), a, b, weight_kv, weight_q, *buffers)


def finish_kernel(nz, place_ref, keep_ref, got_ref, low_ref, high_ref, near_ref, far_ref, *refs):
    outs, acc_ref = refs[:-1], refs[-1]
    first = place_ref[0] == 0

    @pl.when(first)
    def _():
        acc_ref[...] = dot(low_ref[...], far_ref[...], 1, 0)

    @pl.when(jnp.logical_not(first))
    def _():
        acc_ref[...] = dot(high_ref[...], near_ref[...], 1, 0)

    fine = acc_ref.shape[0] // nz
    for steps in range(nz):
        at = pl.multiple_of(lax.rem(place_ref[1] + steps, nz) * fine, 16)
        total = keep_ref[steps, 0].astype(F32) + got_ref[steps, 0].astype(F32)
        part = acc_ref[pl.ds(at, fine), :]
        for h in range(GROUP):
            cols = slice(3 * HEAD * h, 3 * HEAD * h + 2 * HEAD)
            rest = slice(3 * HEAD * h + 2 * HEAD, 3 * HEAD * (h + 1))
            added = total[:, cols] + part[:, 2 * HEAD * h : 2 * HEAD * (h + 1)]
            outs[steps][0, :, cols] = added.astype(BF)
            outs[steps][0, :, rest] = total[:, rest].astype(BF)


def finish(place, nz, keep, got, low, high, near, far):
    rows = D // 8
    shape = (4, rows // nz, COLS)
    both = pl.BlockSpec((nz, 1) + shape[1:], lambda n, place: (0, n, 0, 0))
    part = pl.BlockSpec((rows, low.shape[1]), lambda n, place: (n, 0))
    fixed = pl.BlockSpec(near.shape, lambda n, place: (0, 0))
    return pl.pallas_call(
        lambda *refs: finish_kernel(nz, *refs),
        grid_spec=pltpu.PrefetchScalarGridSpec(
            num_scalar_prefetch=1,
            grid=(4,),
            in_specs=[both, both, part, part, fixed, fixed],
            out_specs=[pl.BlockSpec((1,) + shape[1:], lambda n, place: (n, 0, 0))] * nz,
            scratch_shapes=[pltpu.VMEM((rows, near.shape[1]), F32)],
        ),
        out_shape=[jax.ShapeDtypeStruct(shape, BF)] * nz,
        compiler_params=pltpu.CompilerParams(vmem_limit_bytes=60 * 1024 * 1024),
        cost_estimate=pl.CostEstimate(
            flops=FIRST, bytes_accessed=12 * 1024 * 1024, transcendentals=0
        ),
    )(place, keep, got, low, high, near, far)


def input_kernel(place_ref, dkv_ref, extra_ref, dq_ref, wkv_ref, wq_ref, *refs):
    step = pl.program_id(0)
    late = place_ref[step] >= 2
    extra = jnp.where(late, extra_ref[...].astype(F32), 0.0)
    dkv = (dkv_ref[...].astype(F32) + extra).astype(BF)
    total = dot(dkv, wkv_ref[...], 1, 1) + dot(dq_ref[...], wq_ref[...], 1, 1)
    half = total.shape[0] // 2
    if len(refs) == 1:
        refs[0][...] = total.astype(BF)
        return
    if len(refs) == 2:
        refs[0][...] = total[:half].astype(BF)
        refs[1][...] = total[half:].astype(BF)
        return
    top_ref, low_ref, left_ref, right_ref = refs

    @pl.when(step == 0)
    def _():
        left_ref[:half, :] = (total[:half] + top_ref[...].astype(F32)).astype(BF)
        left_ref[half:, :] = total[half:].astype(BF)

    @pl.when(step == 1)
    def _():
        right_ref[:half, :] = total[:half].astype(BF)
        right_ref[half:, :] = (total[half:] + low_ref[...].astype(F32)).astype(BF)


def input_grads(blocks, dkv, extra, dq, weight_kv, weight_q, heights, work, back=()):
    wide = dq.shape[1]
    tok = dq.shape[0] // 4
    rows = lambda cols: pl.BlockSpec((tok, cols), lambda n, place: (place[n], 0))
    whole = lambda rows, cols: pl.BlockSpec((rows, cols), lambda n, place: (0, 0))
    made = [(height, D) for height in heights]
    return pl.pallas_call(
        input_kernel,
        grid_spec=pltpu.PrefetchScalarGridSpec(
            num_scalar_prefetch=1,
            grid=(len(blocks),),
            in_specs=[
                rows(2 * wide),
                pl.BlockSpec((tok, 2 * wide), lambda n, place: (jnp.maximum(place[n] - 2, 0), 0)),
                rows(wide), whole(D, 2 * wide), whole(D, wide),
            ]
            + [whole(tok // 2, D)] * len(back),
            out_specs=[whole(*shape) for shape in made],
        ),
        out_shape=[jax.ShapeDtypeStruct(shape, BF) for shape in made],
        compiler_params=pltpu.CompilerParams(vmem_limit_bytes=60 * 1024 * 1024),
        cost_estimate=pl.CostEstimate(
            flops=work, bytes_accessed=12 * 1024 * 1024, transcendentals=0
        ),
    )(jnp.stack(blocks), dkv, extra, dq, weight_kv, weight_q, *back)


def block_of(array, index, size):
    return lax.dynamic_slice_in_dim(array, index * size, size, 0)


def put(array, part, index):
    return lax.dynamic_update_slice_in_dim(array, part, index * part.shape[0], 0)


def on_device(sizes, inputs, w_query, w_key, w_value, out_grad):
    c = lax.axis_index("c")
    y = lax.axis_index("y")
    z = lax.axis_index("z")
    xl = lax.axis_index("xl")
    nz, nh = sizes["z"], sizes["xh"]
    tok = inputs.shape[1]
    half = tok // 2
    home = xl == c

    def ring(value, axis, steps, count=4):
        return lax.ppermute(value, axis, [(i, (i + steps) % count) for i in range(count)])

    def side_ring(value, axis, steps, count, own):
        pairs = []
        for side in range(2):
            core = side if own else 1 - side
            for i in range(count):
                j = (i + steps) % count
                pairs.append(((side * count + i) * 2 + core, (side * count + j) * 2 + core))
        return lax.ppermute(value, ("xl", axis, "c"), pairs)

    def swap_sides(value):
        return lax.ppermute(value, ("xl", "c"), [(1, 2), (2, 1)])

    at = lambda steps: (y + steps) % 4
    wide = GROUP * HEAD

    def crossed(value, steps):
        pairs = []
        for side in range(2):
            for i in range(4):
                for core in range(2):
                    there = ((core * 4 + (i + steps) % 4) * 2) + side
                    if steps or side != core:
                        pairs.append(((side * 4 + i) * 2 + core, there))
        return lax.ppermute(value, ("xl", "y", "c"), pairs)

    own = inputs[0]
    moved = swap_sides(own)
    left_home = side_ring(own, "y", 1, 4, True)
    right_home = side_ring(own, "y", -1, 4, True)
    weight_q, weight_kv = pick_weights(y, w_query, w_key, w_value)
    moved, left_home, right_home, weight_q, weight_kv, out_grad = lax.optimization_barrier(
        (moved, left_home, right_home, weight_q, weight_kv, out_grad)
    )
    left_away = side_ring(moved, "y", 1, 4, False)
    right_away = side_ring(moved, "y", -1, 4, False)
    cols = lambda index: lax.dynamic_slice_in_dim(out_grad[0], index * wide, wide, 1)
    dout_own = cols(y)
    dout_own = jnp.where(home, dout_own, crossed(dout_own, 0))
    dout_left = crossed(cols(at(1)), 1)
    dout_right = crossed(cols(at(-1)), -1)
    dout_far = crossed(cols(at(2)), 2)
    buffers = place_block((), own, moved, home, y, weight_kv, weight_q)
    dout_all = jnp.zeros((4 * tok, wide), BF)
    for part, index in ((dout_far, at(2)), (dout_left, at(-1)), (dout_right, at(1)), (dout_own, y)):
        dout_all = put(dout_all, part, index)
    buffers, dout_all, left_away, right_away = lax.optimization_barrier(
        (buffers, dout_all, left_away, right_away)
    )
    far_top, far_low = choose(home, left_home, left_away, right_home, right_away)
    far_top = ring(far_top, "y", 1)
    far_low = ring(far_low, "y", -1)
    buffers = place_block(buffers, left_home, left_away, home, at(-1), weight_kv, weight_q)
    buffers = place_block(buffers, right_home, right_away, home, at(1), weight_kv, weight_q)
    tokens, kv, q = place_block(
        buffers, far_top, far_low, home, at(2), weight_kv, weight_q, split=True
    )

    halo = lax.ppermute(kv[2 * tok :], "c", [(0, 1)])
    bias = jnp.where(c == 0, -1e30, 0.0).astype(F32).reshape(1, 1)
    mine = jnp.stack([c, z])
    dq, dkv, dhalo, give, keep, low, high = attention(
        mine, bias, q, kv, halo, dout_all, tokens, nz
    )
    far_dhalo = lax.ppermute(dhalo, "c", [(1, 0)])
    got = lax.ppermute(give, "c", [(0, 1), (1, 0)])
    high = lax.ppermute(high, "c", [(0, 1)])
    far_parts = input_grads(
        [at(2)], dkv, far_dhalo, dq, weight_kv, weight_q, (half, half), FIRST
    )
    back_top = ring(far_parts[0], "y", -1)
    back_low = ring(far_parts[1], "y", 1)
    keep, far_parts = lax.optimization_barrier((keep, far_parts))
    slabs = list(finish(mine, nz, keep, got, low, high, dhalo, far_dhalo))
    sent = [ring(slabs[steps], "z", steps, nz) for steps in range(1, nz)]
    dkv, slabs[0] = lax.optimization_barrier((dkv, slabs[0]))
    part_left, part_right = input_grads(
        [at(-1), at(1)], dkv, far_dhalo, dq, weight_kv, weight_q, (tok, tok), FIRST,
        (back_top, back_low),
    )
    from_right = ring(part_left, "y", -1)
    from_left = ring(part_right, "y", 1)
    *sent, part_left = lax.optimization_barrier((*sent, part_left))
    share = slabs[0].astype(F32)
    for part in sent:
        share = share + part.astype(F32)
    share = share.astype(BF)

    dkv, share = lax.optimization_barrier((dkv, share))
    (part_own,) = input_grads(
        [y], dkv, far_dhalo, dq, weight_kv, weight_q, (tok,), 2 * tok * D * COLS
    )
    around = 2 * nh
    arrived = []
    for steps in range(1, around):
        pairs = []
        for core in range(2):
            for xh in range(nh):
                source = (xh * 2 + core + steps) % around
                pairs.append(
                    (((source % 2) * nh + source // 2) * 2 + core, (core * nh + xh) * 2 + core)
                )
        arrived.append(lax.ppermute(share, ("xl", "xh", "c"), pairs))
    *arrived, from_left, from_right = lax.optimization_barrier((*arrived, from_left, from_right))
    summed = share.astype(F32)
    for part in arrived:
        summed = summed + part.astype(F32)
    summed = summed.astype(BF)
    input_grad = part_own.astype(F32) + from_right.astype(F32) + from_left.astype(F32)
    input_grad = input_grad.astype(BF)
    away_grad = swap_sides(input_grad)

    fine = D // 8 // nz
    piece = lambda index: lax.dynamic_index_in_dim(summed, index % 4, 0, keepdims=False)
    gathered = jnp.zeros((3, fine, D), BF)

    def spread(gathered, piece, index):
        column = lambda i: piece[:, i * HEAD : (i + 1) * HEAD]
        parts = [[column(3 * h + part) for h in range(GROUP)] for part in (2, 0, 1)]
        parts = jnp.stack([jnp.concatenate(part, axis=1) for part in parts])
        return lax.dynamic_update_slice_in_dim(gathered, parts, index * wide, 2)

    gathered = spread(gathered, piece(y), y)
    for steps in range(1, 4):
        gathered = spread(gathered, side_ring(piece(y + steps), "y", steps, 4, True), at(-steps))
    result = jnp.zeros((3, nz * fine, D), BF)
    result = lax.dynamic_update_slice_in_dim(result, gathered, z * fine, 1)
    for steps in range(1, nz):
        result = lax.dynamic_update_slice_in_dim(
            result, side_ring(gathered, "z", steps, nz, True), (z - steps) % nz * fine, 1
        )
    result, away_grad = lax.optimization_barrier((result, away_grad))
    other = lax.ppermute(result, ("xl", "c"), [(0, 1), (3, 2)])
    input_grad = jnp.where(home, input_grad, away_grad)
    outs = [jnp.where(home, result[part], other[part]).astype(F32) for part in range(3)]
    return input_grad[None], outs[0], outs[1], outs[2]


def solution(mesh):
    dp = mesh.shape["dp"]
    nz = 4 if dp == 16 else 1
    nh = dp // 2 // nz
    sizes = {"xl": 2, "y": 4, "xh": nh, "z": nz, "c": 2}
    fine = Mesh(mesh.devices.reshape(tuple(sizes.values())), tuple(sizes))
    block, rollouts = ("xl", "y"), ("xh", "z", "c")
    placed = (P(rollouts, block, None), P(), P(), P(), P(rollouts, block, None))
    return jax.shard_map(
        lambda *arrays: on_device(sizes, *arrays),
        mesh=fine,
        in_specs=placed,
        out_specs=(P(rollouts, block, None), P(block, None), P(block, None), P(block, None)),
        check_vma=False,
    )
```
